512 devices in a mesh: ctx: 64 (over z_lo, y, x), tp: 8 (over z_hi, core).
Axes of the slice: x: 4, y: 4, z: 16 (z_hi: 4, z_lo: 4; z = z_hi * 4 + z_lo), core: 2. Of those that a mesh axis runs over, the one named last changes fastest.
Arguments:
- query: bfloat16 [32768, 4096], P(('ctx', 'tp')), may hold values from -6 to 6
- key_states: bfloat16 [32768, 1024], P(('ctx', 'tp')), may hold values from -6 to 6
- value_states: bfloat16 [32768, 1024], P(('ctx', 'tp')), may hold values from -6 to 6
- grad_out: bfloat16 [32768, 4096], P(('ctx', 'tp')), may hold values from -6 to 6
- segment_ids: int32 [32768], replicated, may hold values from 0 to 34, as said below
Outputs:
- attention_out: bfloat16 [32768, 4096], P('ctx', 'tp')
- query_grad: bfloat16 [32768, 4096], P('ctx', 'tp')
- key_grad: bfloat16 [32768, 1024], P('ctx', 'tp')
- value_grad: bfloat16 [32768, 1024], P('ctx', 'tp')
The draws below stay inside these ranges and needn't reach their ends.
Inputs may be any that keep to these rules, and one draw needn't show every extreme that they name: `segment_ids`: never falling along the tokens, starting at 0 and rising by one at each new document; every document has 1 to 1024 tokens, and one has exactly 1024.
All inputs are finite; a program needn't handle non-finite values.
Results may differ from the reference program's by a relative error of at most 0.035.
Values may be sent and summed in bfloat16 or wider, within the bound.
A program may use at most 64 MiB of HBM per device.

```python
import jax
import jax.numpy as jnp
from jax import lax

QH = 32
KVH = 8
HD = 128
TOK_DEV = 512
TOKENS = 32768


def draw_query(key, part):
    key = jax.random.fold_in(key, 11)
    entries = jnp.clip(jax.random.normal(key, (TOKENS, QH * HD), jnp.float32), -6.0, 6.0)
    return entries.astype(jnp.bfloat16)


def draw_key_states(key, part):
    key = jax.random.fold_in(key, 23)
    entries = jnp.clip(jax.random.normal(key, (TOKENS, KVH * HD), jnp.float32), -6.0, 6.0)
    return entries.astype(jnp.bfloat16)


def draw_segment_ids(key, part):
    key = jax.random.fold_in(key, 37)
    blocks = TOKENS // TOK_DEV
    start = jax.random.randint(jax.random.fold_in(key, 1), (), 1, TOK_DEV // 2 + 1).astype(jnp.int32)
    cut = jax.random.randint(jax.random.fold_in(key, 2), (), 1, TOK_DEV).astype(jnp.int32)
    places = jnp.arange(TOKENS, dtype=jnp.int32)
    filler_start = (blocks - 4) * TOK_DEV + start
    long_starts = (places >= start) & ((places - start) % (2 * TOK_DEV) == 0) & (places <= filler_start)
    flags = (places == 0) | long_starts | (places == filler_start + cut)
    flags = flags | (places == (blocks - 3) * TOK_DEV + start) | (places == (blocks - 1) * TOK_DEV + start)
    return (jnp.cumsum(flags.astype(jnp.int32)) - 1).astype(jnp.int32)


def block_levels(own_key, extent, shards, smallest, largest):
    factor_of, own = 1.0, jax.random.fold_in(own_key, 6)
    for axis_at, shards_of in shards:
        draws = jnp.exp(jax.random.uniform(jax.random.fold_in(own, axis_at), (shards_of,), jnp.float32, smallest / len(shards), largest / len(shards)))
        factor_of = factor_of * jnp.repeat(draws, extent[axis_at] // shards_of).reshape([-1 if axis == axis_at else 1 for axis in range(len(extent))])
    return factor_of


def gaussian(key, dims, deviation, most, split=(), kind=jnp.bfloat16):
    values = jax.random.normal(key, dims, jnp.float32) * deviation
    if len(split) > 0:
        values = block_levels(key, dims, split, -0.22, 0.18) * values
    return jnp.clip(values, min=-most, max=most).astype(kind)


def setup_inputs(seed: int = 0) -> dict:
    splits = jax.random.split(jax.random.key(seed), 6)
    query = draw_query(jax.random.fold_in(splits[5], 71), 0)
    key_states = draw_key_states(jax.random.fold_in(splits[5], 71), 0)
    value_states = gaussian(splits[2], (TOKENS, KVH * HD), 1.0, 6.0, ((0, 512),))
    grad_out = gaussian(splits[3], (TOKENS, QH * HD), 1.0, 6.0, ((0, 512),))
    segment_ids = draw_segment_ids(jax.random.fold_in(splits[5], 71), 0)
    return {"query": query, "key_states": key_states, "value_states": value_states, "grad_out": grad_out, "segment_ids": segment_ids}


NEGATIVE = -1e30


def reference(query, key_states, value_states, grad_out, segment_ids):
    scaling = HD ** -0.5
    group_size = QH // KVH
    margin = 2 * TOK_DEV
    window = 3 * TOK_DEV
    key_padded = jnp.concatenate([jnp.zeros((margin, KVH * HD), key_states.dtype), key_states], 0)
    value_padded = jnp.concatenate([jnp.zeros((margin, KVH * HD), value_states.dtype), value_states], 0)
    segs_whole = segment_ids.astype(jnp.int32)
    segs_padded = jnp.concatenate([jnp.full((margin,), -1, jnp.int32), segs_whole])
    row_places = jnp.arange(TOK_DEV, dtype=jnp.int32) + margin
    col_places = jnp.arange(window, dtype=jnp.int32)

    def one_block(block):
        offset = (block * TOK_DEV).astype(jnp.int32)
        queries = lax.dynamic_slice_in_dim(query, offset, TOK_DEV, 0).reshape(TOK_DEV, QH, HD).astype(jnp.float32)
        grads = lax.dynamic_slice_in_dim(grad_out, offset, TOK_DEV, 0).reshape(TOK_DEV, QH, HD).astype(jnp.float32)
        keys_win = lax.dynamic_slice_in_dim(key_padded, offset, window, 0).reshape(window, KVH, HD)
        values_win = lax.dynamic_slice_in_dim(value_padded, offset, window, 0).reshape(window, KVH, HD)
        keys_rep = jnp.repeat(keys_win, group_size, axis=1).astype(jnp.float32)
        values_rep = jnp.repeat(values_win, group_size, axis=1).astype(jnp.float32)
        key_segs = lax.dynamic_slice_in_dim(segs_padded, offset, window, 0)
        query_segs = lax.dynamic_slice_in_dim(segs_whole, offset, TOK_DEV, 0)
        allowed = (query_segs[:, None] == key_segs[None, :]) & (col_places[None, :] <= row_places[:, None])
        scores = jnp.einsum('qhd,khd->hqk', queries, keys_rep) * scaling
        scores = jnp.where(allowed[None], scores, NEGATIVE)
        peak = jnp.max(scores, axis=-1, keepdims=True)
        expos = jnp.exp(scores - peak)
        probs = expos / jnp.sum(expos, axis=-1, keepdims=True)
        probs_half = probs.astype(jnp.bfloat16)
        attended = jnp.einsum('hqk,khd->qhd', probs_half.astype(jnp.float32), values_rep).astype(jnp.bfloat16)
        row_delta = jnp.sum(grads * attended.astype(jnp.float32), axis=-1).T
        grad_probs = jnp.einsum('qhd,khd->hqk', grads, values_rep)
        slopes = (probs * (grad_probs - row_delta[:, :, None])).astype(jnp.bfloat16).astype(jnp.float32)
        query_part = (jnp.einsum('hqk,khd->qhd', slopes, keys_rep) * scaling).astype(jnp.bfloat16)
        key_part = jnp.einsum('hqk,qhd->khd', slopes, queries) * scaling
        value_part = jnp.einsum('hqk,qhd->khd', probs_half.astype(jnp.float32), grads)
        key_part = jnp.sum(key_part.reshape(window, KVH, group_size, HD), axis=2).reshape(window, KVH * HD)
        value_part = jnp.sum(value_part.reshape(window, KVH, group_size, HD), axis=2).reshape(window, KVH * HD)
        return attended.reshape(TOK_DEV, QH * HD), query_part.reshape(TOK_DEV, QH * HD), key_part, value_part

    block_count = TOKENS // TOK_DEV
    attended_all, query_all, key_windows, value_windows = lax.map(one_block, jnp.arange(block_count, dtype=jnp.int32))

    def combine(windows):
        pieces = windows.reshape(block_count, 3, TOK_DEV, KVH * HD)
        filler = jnp.zeros((2, TOK_DEV, KVH * HD), windows.dtype)
        near_terms = jnp.concatenate([pieces[1:, 1], filler[:1]], 0)
        far_terms = jnp.concatenate([pieces[2:, 0], filler], 0)
        total = pieces[:, 2] + near_terms + far_terms
        return total.reshape(TOKENS, KVH * HD).astype(jnp.bfloat16)

    attention_out = attended_all.reshape(TOKENS, QH * HD)
    query_grad = query_all.reshape(TOKENS, QH * HD)
    return attention_out, query_grad, combine(key_windows), combine(value_windows)
```

```python
import math

import jax
import jax.numpy as jnp
from jax import lax
from jax.experimental import pallas as pl
from jax.experimental.pallas import tpu as pltpu
from jax.sharding import PartitionSpec as P

QH = 32
KVH = 8
HD = 128
TOK = 512
SUB = 64
GROUP = QH // KVH
CTX = 64
TP = 8
LANES = SUB * GROUP
WIN = 1152
TILE = 128
TILES = WIN // TILE
NEGATIVE = -1e30
MESH = pl.DeviceIdType.MESH
SCALING = HD**-0.5
EXP_SCALE = SCALING * math.log2(math.e)

NT = (((1,), (1,)), ((), ()))


def dot(a, b):
    return jnp.dot(a, b, preferred_element_type=jnp.float32)


def dot_nt(a, b):
    return lax.dot_general(a, b, NT, preferred_element_type=jnp.float32)


def fold(x, op):
    parts = [x[i * 8 : (i + 1) * 8] for i in range(x.shape[0] // 8)]
    while len(parts) > 1:
        parts = [op(parts[i], parts[i + 1]) for i in range(0, len(parts), 2)]
    return parts[0]


def kernel(
    q_in,
    k_in,
    v_in,
    g_in,
    seg_in,
    out_ref,
    dq_ref,
    dk_ref,
    dv_ref,
    qbuf,
    gbuf,
    kv,
    kvt,
    segcol,
    segrow,
    s_scr,
    p_scr,
    e_scr,
    acc,
    tx,
    rx,
    q_send,
    q_recv,
    g_send,
    g_recv,
    k_send,
    k_recv,
    v_send,
    v_recv,
    w_send,
    w_recv,
    t_send,
    t_recv,
):
    c = lax.axis_index("ctx")
    t = lax.axis_index("tp")
    zh, co = t // 2, t % 2

    barrier = pltpu.get_barrier_semaphore()
    for d in range(1, TP):
        pl.semaphore_signal(barrier, inc=1, device_id={"tp": (t + d) % TP}, device_id_type=MESH)
    for d in (1, 2, CTX - 1, CTX - 2):
        pl.semaphore_signal(barrier, inc=1, device_id={"ctx": (c + d) % CTX}, device_id_type=MESH)

    def narrow(ref, j):
        return ref.at[:, pl.ds(pl.multiple_of(j * HD, HD), HD)]

    def wide(ref, j):
        return ref.at[:, pl.ds(pl.multiple_of(j * GROUP * HD, GROUP * HD), GROUP * HD)]

    def own_rows(j):
        return pl.ds(pl.multiple_of(2 * TOK + j * SUB, SUB), SUB)

    pltpu.make_async_copy(narrow(k_in, t), kv.at[0, own_rows(t)], k_recv.at[t]).start()
    pltpu.make_async_copy(narrow(v_in, t), kv.at[1, own_rows(t)], v_recv.at[t]).start()
    pltpu.make_async_copy(wide(q_in, t), qbuf.at[t], q_recv.at[t]).start()
    pltpu.make_async_copy(wide(g_in, t), gbuf.at[t], g_recv.at[t]).start()

    @pl.when(c < 1)
    def _():
        kv[:, TOK : 2 * TOK] = jnp.zeros((2, TOK, HD), jnp.bfloat16)

    @pl.when(c < 2)
    def _():
        kv[:, 0:TOK] = jnp.zeros((2, TOK, HD), jnp.bfloat16)

    acc[...] = jnp.zeros_like(acc)

    for block in range(3):
        at = jnp.maximum(c - 2 + block, 0)
        rows = seg_in[pl.ds(pl.multiple_of(at * 4, 4), 4), :].astype(jnp.float32)
        rows = jnp.where(c - 2 + block >= 0, rows, -1.0)
        for i in range(4):
            wide_row = jnp.broadcast_to(rows[i : i + 1], (TILE, TILE))
            start = block * TOK + i * TILE
            segcol[start : start + TILE, :] = wide_row.T
    own = seg_in[pl.ds(pl.multiple_of(c * 4, 4), 4), :].astype(jnp.float32)
    low_lane = lax.broadcasted_iota(jnp.int32, (8, TILE), 1) < SUB
    for i in range(4):
        row = jnp.broadcast_to(own[i : i + 1], (8, TILE))
        turned = pltpu.roll(row, SUB, 1)
        low = jnp.where(low_lane, row, turned)
        high = jnp.where(low_lane, turned, row)
        segrow[2 * i] = jnp.concatenate([low, low], 1)
        segrow[2 * i + 1] = jnp.concatenate([high, high], 1)

    pl.semaphore_wait(barrier, TP - 1 + 4)

    def partner(dz, dc):
        return ((zh + dz) % 4) * 2 + (co + dc) % 2

    partners = [(1, 0), (3, 0), (1, 1), (3, 1), (2, 0), (2, 1), (0, 1)]

    def exchange(src, dst, send, recv, to):
        return pltpu.make_async_remote_copy(
            src_ref=src,
            dst_ref=dst,
            send_sem=send.at[to],
            recv_sem=recv.at[t],
            device_id={"tp": to},
            device_id_type=MESH,
        )

    def key_copies(to):
        return (
            exchange(narrow(k_in, to), kv.at[0, own_rows(t)], k_send, k_recv, to),
            exchange(narrow(v_in, to), kv.at[1, own_rows(t)], v_send, v_recv, to),
        )

    def query_copies(to):
        return (
            exchange(wide(q_in, to), qbuf.at[t], q_send, q_recv, to),
            exchange(wide(g_in, to), gbuf.at[t], g_send, g_recv, to),
        )

    for dz, dc in partners:
        for copy in key_copies(partner(dz, dc)):
            copy.start()
    for dz, dc in partners:
        for copy in query_copies(partner(dz, dc)):
            copy.start()

    def wait_key(j, carry):
        pltpu.make_async_copy(kv.at[0, own_rows(j)], kv.at[0, own_rows(j)], k_recv.at[j]).wait()
        pltpu.make_async_copy(kv.at[1, own_rows(j)], kv.at[1, own_rows(j)], v_recv.at[j]).wait()
        return carry

    lax.fori_loop(0, TP, wait_key, 0)

    def window_copy(d):
        return pltpu.make_async_remote_copy(
            src_ref=kv.at[:, pl.ds(2 * TOK, TOK)],
            dst_ref=kv.at[:, pl.ds((2 - d) * TOK, TOK)],
            send_sem=w_send.at[d - 1],
            recv_sem=w_recv.at[d - 1],
            device_id={"ctx": (c + d) % CTX},
            device_id_type=MESH,
        )

    for d in (1, 2):

        @pl.when(c < CTX - d)
        def _():
            window_copy(d).start()

    def turn(start):
        for i in range(TOK // TILE):
            at = start + i * TILE
            for w in range(2):
                block = kv[w, at : at + TILE, :].astype(jnp.float32)
                kvt[w, :, at : at + TILE] = block.T.astype(jnp.bfloat16)

    turn(2 * TOK)
    for d in (1, 2):

        @pl.when(c >= d)
        def _():
            window_copy(d).wait_recv()

        turn((2 - d) * TOK)

    lane = lax.broadcasted_iota(jnp.int32, (TILE, LANES), 1) % SUB
    place = lax.broadcasted_iota(jnp.int32, (TILE, LANES), 0)

    def unit(i, carry):
        a = i // 2
        dz = a + a // 2 - 2 * (a // 3)
        sz, sc = (zh + dz) % 4, (co + i) % 2
        j = sz * 2 + sc
        pltpu.make_async_copy(qbuf.at[j], qbuf.at[j], q_recv.at[j]).wait()
        pltpu.make_async_copy(gbuf.at[j], gbuf.at[j], g_recv.at[j]).wait()
        base = pl.multiple_of(sz * TILE, TILE)

        def keys(n):
            return pl.ds(pl.multiple_of(base + n * TILE, TILE), TILE)

        qs = jnp.concatenate([qbuf[j, :, h * HD : (h + 1) * HD] for h in range(GROUP)], 0)
        gs = jnp.concatenate([gbuf[j, :, h * HD : (h + 1) * HD] for h in range(GROUP)], 0)
        seg_q = segrow[j][0:1]
        causal = place <= lane + sc * SUB

        peak = None
        for n in range(TILES):
            s = dot_nt(kv[0, keys(n), :], qs)
            seg_k = segcol[keys(n), :]
            allowed = jnp.concatenate([seg_k, seg_k], 1) == seg_q
            if n == TILES - 1:
                allowed = allowed & causal
            s = jnp.where(allowed, s, NEGATIVE)
            s_scr[n * TILE : (n + 1) * TILE, :] = s
            here = fold(s, jnp.maximum)
            peak = here if peak is None else jnp.maximum(peak, here)
        peak = jnp.max(peak, axis=0, keepdims=True) * EXP_SCALE

        total = None
        for n in range(TILES):
            p = jnp.exp2(s_scr[n * TILE : (n + 1) * TILE, :] * EXP_SCALE - peak)
            p_scr[n * TILE : (n + 1) * TILE, :] = p.astype(jnp.bfloat16)
            here = fold(p, jnp.add)
            total = here if total is None else total + here
        inverse = 1.0 / jnp.sum(total, axis=0, keepdims=True)

        window = pl.ds(base, WIN)
        attended = dot(kvt[1, :, window], p_scr[...]) * inverse
        gst = gs.astype(jnp.float32).T * inverse
        gst = gst.astype(jnp.bfloat16)
        delta = jnp.sum(gst.astype(jnp.float32) * attended, axis=0, keepdims=True)
        rows = pl.ds(pl.multiple_of(j * SUB, SUB), SUB)

        def store(ref, value):
            value = value.T.astype(jnp.bfloat16)
            for h in range(GROUP):
                ref[rows, h * HD : (h + 1) * HD] = value[h * SUB : (h + 1) * SUB]

        store(out_ref, attended)
        for n in range(TILES):
            p = p_scr[n * TILE : (n + 1) * TILE, :]
            slope = dot(kv[1, keys(n), :], gst)
            e = (p.astype(jnp.float32) * (slope - delta)).astype(jnp.bfloat16)
            e_scr[n * TILE : (n + 1) * TILE, :] = e
            acc[0, keys(n), :] += dot(e, qs)
            acc[1, keys(n), :] += dot_nt(p, gst)
        store(dq_ref, dot(kvt[0, :, window], e_scr[...]) * SCALING)
        return carry

    lax.fori_loop(0, TP, unit, 0)

    def term_copy(d):
        return pltpu.make_async_remote_copy(
            src_ref=tx.at[d - 1],
            dst_ref=rx.at[d - 1],
            send_sem=t_send.at[d - 1],
            recv_sem=t_recv.at[d - 1],
            device_id={"ctx": (c + CTX - d) % CTX},
            device_id_type=MESH,
        )

    for d in (2, 1):
        at = (2 - d) * TOK
        tx[d - 1, 0] = (acc[0, at : at + TOK, :] * SCALING).astype(jnp.bfloat16)
        tx[d - 1, 1] = acc[1, at : at + TOK, :].astype(jnp.bfloat16)

        @pl.when(c >= d)
        def _():
            term_copy(d).start()

    for d in (2, 1):

        @pl.when(c < CTX - d)
        def _():
            term_copy(d).wait_recv()

        @pl.when(c >= CTX - d)
        def _():
            rx[d - 1] = jnp.zeros((2, TOK, HD), jnp.bfloat16)

    for w, ref in ((0, dk_ref), (1, dv_ref)):
        own_sum = acc[w, 2 * TOK : 3 * TOK, :]
        if w == 0:
            own_sum = own_sum * SCALING
        ref[...] = (
            own_sum + rx[0, w].astype(jnp.float32) + rx[1, w].astype(jnp.float32)
        ).astype(jnp.bfloat16)

    for dz, dc in partners:
        for copy in key_copies(partner(dz, dc)) + query_copies(partner(dz, dc)):
            copy.wait_send()
    for d in (1, 2):

        @pl.when(c < CTX - d)
        def _():
            window_copy(d).wait_send()

        @pl.when(c >= d)
        def _():
            term_copy(d).wait_send()


def on_device(query, key_states, value_states, grad_out, segment_ids):
    vmem = pl.BlockSpec(memory_space=pltpu.VMEM)
    hbm = pl.BlockSpec(memory_space=pl.ANY)
    bf16, f32 = jnp.bfloat16, jnp.float32
    dma = pltpu.SemaphoreType.DMA
    return pl.pallas_call(
        kernel,
        out_shape=(
            jax.ShapeDtypeStruct((TOK, GROUP * HD), bf16),
            jax.ShapeDtypeStruct((TOK, GROUP * HD), bf16),
            jax.ShapeDtypeStruct((TOK, HD), bf16),
            jax.ShapeDtypeStruct((TOK, HD), bf16),
        ),
        in_specs=[hbm, hbm, hbm, hbm, vmem],
        out_specs=(vmem, vmem, vmem, vmem),
        scratch_shapes=[
            pltpu.VMEM((TP, SUB, GROUP * HD), bf16),
            pltpu.VMEM((TP, SUB, GROUP * HD), bf16),
            pltpu.VMEM((2, 3 * TOK, HD), bf16),
            pltpu.VMEM((2, HD, 3 * TOK), bf16),
            pltpu.VMEM((3 * TOK, TILE), f32),
            pltpu.VMEM((TP, 8, LANES), f32),
            pltpu.VMEM((WIN, LANES), f32),
            pltpu.VMEM((WIN, LANES), bf16),
            pltpu.VMEM((WIN, LANES), bf16),
            pltpu.VMEM((2, 3 * TOK, HD), f32),
            pltpu.VMEM((2, 2, TOK, HD), bf16),
            pltpu.VMEM((2, 2, TOK, HD), bf16),
        ]
        + [dma((TP,))] * 8
        + [dma((2,))] * 4,
        compiler_params=pltpu.CompilerParams(
            collective_id=0, has_side_effects=True, vmem_limit_bytes=32 * 2**20
        ),
        cost_estimate=pl.CostEstimate(
            flops=2 * 6 * TP * LANES * WIN * HD,
            bytes_accessed=4 * TOK * GROUP * HD * 2,
            transcendentals=TP * LANES * WIN,
        ),
        name="attention",
    )(query, key_states, value_states, grad_out, segment_ids.reshape(-1, TILE))


def solution(mesh):
    in_specs = (
        P(("ctx", "tp"), None),
        P(("ctx", "tp"), None),
        P(("ctx", "tp"), None),
        P(("ctx", "tp"), None),
        P(),
    )
    out_specs = (P("ctx", "tp"), P("ctx", "tp"), P("ctx", "tp"), P("ctx", "tp"))
    return jax.shard_map(
        on_device, mesh=mesh, in_specs=in_specs, out_specs=out_specs, check_vma=False
    )
```

```python
import math

import jax
import jax.numpy as jnp
from jax import lax
from jax.experimental import pallas as pl
from jax.experimental.pallas import tpu as pltpu
from jax.sharding import PartitionSpec as P

QH = 32
KVH = 8
HD = 128
TOK = 512
SUB = 64
GROUP = QH // KVH
CTX = 64
PLANE = 16
PLANES = CTX // PLANE
EARLY = 2
TP = 8
LANES = SUB * GROUP
WIN = 1152
TILE = 128
TILES = WIN // TILE
NEGATIVE = -1e30
MESH = pl.DeviceIdType.MESH
SCALING = HD**-0.5
EXP_SCALE = SCALING * math.log2(math.e)

PARTS = ((2, 0, TOK // 2), (2, TOK // 2, TOK // 2), (1, TOK, TOK))

NT = (((1,), (1,)), ((), ()))


def dot(a, b):
    return jnp.dot(a, b, preferred_element_type=jnp.float32)


def dot_nt(a, b):
    return lax.dot_general(a, b, NT, preferred_element_type=jnp.float32)


def fold(x, op):
    parts = [x[i * 8 : (i + 1) * 8] for i in range(x.shape[0] // 8)]
    while len(parts) > 1:
        parts = [op(parts[i], parts[i + 1]) for i in range(0, len(parts), 2)]
    return parts[0]


def kernel(
    q_in,
    k_in,
    v_in,
    g_in,
    seg_in,
    out_ref,
    dq_ref,
    dk_ref,
    dv_ref,
    q_vm,
    g_vm,
    k_vm,
    v_vm,
    kv_out,
    qg_out,
    qg,
    kv,
    kvt,
    segcol,
    segrow,
    s_scr,
    p_scr,
    e_scr,
    acc,
    tx,
    rx,
    load_sem,
    q_send,
    q_recv,
    k_send,
    k_recv,
    w_send,
    w_recv,
    t_send,
    t_recv,
    seg,
    relay,
    seg_sem,
    r_send,
    r_recv,
    x_send,
    x_recv,
):
    c = lax.axis_index("ctx")
    t = lax.axis_index("tp")
    zh, co = t // 2, t % 2
    plane, p = c // PLANE, c % PLANE

    seg_copy = pltpu.make_async_copy(seg_in, seg, seg_sem)
    seg_copy.start()
    loads = [
        pltpu.make_async_copy(k_in, k_vm, load_sem.at[0]),
        pltpu.make_async_copy(v_in, v_vm, load_sem.at[1]),
        pltpu.make_async_copy(q_in, q_vm, load_sem.at[2]),
        pltpu.make_async_copy(g_in, g_vm, load_sem.at[3]),
    ]
    for load in loads:
        load.start()

    barrier = pltpu.get_barrier_semaphore()
    for d in range(1, TP):
        pl.semaphore_signal(barrier, inc=1, device_id={"tp": (t + d) % TP}, device_id_type=MESH)
    for d in (1, 2, CTX - 1, CTX - 2):
        pl.semaphore_signal(barrier, inc=1, device_id={"ctx": (c + d) % CTX}, device_id_type=MESH)

    crossing = plane < PLANES - 1

    def greet(block, to=t):
        pl.semaphore_signal(
            barrier, inc=1, device_id={"ctx": block, "tp": to}, device_id_type=MESH
        )

    first = plane * PLANE

    @pl.when(p < 8)
    def _():
        greet(first + 15)

    @pl.when((p >= 8) & (p != 14))
    def _():
        greet(first + 14)

    @pl.when(p == 15)
    def _():
        for r in range(TP):
            greet(first + r)

    @pl.when(p == 14)
    def _():
        for r in range(TP):
            if r != 6:
                greet(first + 8 + r)

    @pl.when((p == 0) & (plane >= 1))
    def _():
        for r in range(TP):
            greet(first - PLANE + t, r)
            greet(first - PLANE + 8 + t, r)

    arrivals = (
        TP - 1 + 4 + jnp.where(p < 14, 1, jnp.where(p == 14, 7, 9)) + jnp.where(crossing, 1, 0)
    )

    def own_rows(j):
        return pl.ds(pl.multiple_of(2 * TOK + j * SUB, SUB), SUB)

    for load in loads:
        load.wait()
    for j in range(TP):
        kv_out[j, 0] = k_vm[:, j * HD : (j + 1) * HD]
        kv_out[j, 1] = v_vm[:, j * HD : (j + 1) * HD]
    for j in range(TP):
        for h in range(GROUP):
            at = (j * GROUP + h) * HD
            qg_out[j, h] = q_vm[:, at : at + HD]
            qg_out[j, GROUP + h] = g_vm[:, at : at + HD]

    @pl.when(c < 1)
    def _():
        kv[:, TOK : 2 * TOK] = jnp.zeros((2, TOK, HD), jnp.bfloat16)

    @pl.when(c < 2)
    def _():
        kv[:, 0:TOK] = jnp.zeros((2, TOK, HD), jnp.bfloat16)

    kv[:, own_rows(t), :] = kv_out[t]
    qg[t] = qg_out[t]
    acc[...] = jnp.zeros_like(acc)

    seg_copy.wait()
    for block in range(3):
        at = jnp.maximum(c - 2 + block, 0)
        rows = seg[pl.ds(pl.multiple_of(at * 4, 4), 4), :].astype(jnp.float32)
        rows = jnp.where(c - 2 + block >= 0, rows, -1.0)
        for i in range(4):
            wide_row = jnp.broadcast_to(rows[i : i + 1], (TILE, TILE))
            start = block * TOK + i * TILE
            segcol[start : start + TILE, :] = wide_row.T
    own = seg[pl.ds(pl.multiple_of(c * 4, 4), 4), :].astype(jnp.float32)
    low_lane = lax.broadcasted_iota(jnp.int32, (8, TILE), 1) < SUB
    for i in range(4):
        row = jnp.broadcast_to(own[i : i + 1], (8, TILE))
        turned = pltpu.roll(row, SUB, 1)
        low = jnp.where(low_lane, row, turned)
        high = jnp.where(low_lane, turned, row)
        segrow[2 * i] = jnp.concatenate([low, low], 1)
        segrow[2 * i + 1] = jnp.concatenate([high, high], 1)

    pl.semaphore_wait(barrier, arrivals)

    def partner(dz, dc):
        return ((zh + dz) % 4) * 2 + (co + dc) % 2

    partners = [(1, 0), (3, 0), (1, 1), (3, 1), (2, 0), (2, 1), (0, 1)]
    to_1, to_2, to_3 = (zh + 1) % 4, (zh + 3) % 4, (zh + 2) % 4
    targets = [to_1 * 2 + co, to_2 * 2 + co, to_1 * 2 + 1 - co, to_2 * 2 + 1 - co]
    targets += [zh * 2 + 1 - co, to_3 * 2 + co, to_3 * 2 + 1 - co]

    def exchange(src, dst, send, recv, to):
        return pltpu.make_async_remote_copy(
            src_ref=src,
            dst_ref=dst,
            send_sem=send.at[to],
            recv_sem=recv.at[t],
            device_id={"tp": to},
            device_id_type=MESH,
        )

    def key_copy(to):
        return exchange(kv_out.at[to], kv.at[:, own_rows(t)], k_send, k_recv, to)

    def query_copy(to):
        return exchange(qg_out.at[to], qg.at[t], q_send, q_recv, to)

    def relay_copy(r):
        return pltpu.make_async_remote_copy(
            src_ref=kv_out.at[r],
            dst_ref=relay,
            send_sem=r_send.at[r],
            recv_sem=r_recv,
            device_id={"ctx": first + r + 8 * (15 - p)},
            device_id_type=MESH,
        )

    def cross_copy(src):
        at = jnp.where(p < 8, TOK, 0) + t * SUB
        return pltpu.make_async_remote_copy(
            src_ref=src,
            dst_ref=kv.at[:, pl.ds(pl.multiple_of(at, SUB), SUB)],
            send_sem=x_send,
            recv_sem=x_recv.at[jnp.where(p < 8, 0, 8) + t],
            device_id={"ctx": (plane + 1) % PLANES * PLANE, "tp": p % 8},
            device_id_type=MESH,
        )

    @pl.when((p == 15) & crossing)
    def _():
        for r in range(TP):
            relay_copy(r).start()

    @pl.when((p == 14) & crossing)
    def _():
        for r in range(TP):
            if r != 6:
                relay_copy(r).start()
        cross_copy(kv_out.at[6]).start()

    for dz, dc in partners:
        key_copy(partner(dz, dc)).start()

    @pl.when((p != 14) & crossing)
    def _():
        pltpu.make_async_copy(relay, relay, r_recv).wait()
        cross_copy(relay).start()

    for to in targets[:EARLY]:
        query_copy(to).start()

    for dz, dc in partners:
        j = partner(dz, dc)
        rows = kv.at[:, own_rows(j)]
        pltpu.make_async_copy(rows, rows, k_recv.at[j]).wait()

    def window_copy(d):
        return pltpu.make_async_remote_copy(
            src_ref=kv.at[:, pl.ds(2 * TOK, TOK)],
            dst_ref=kv.at[:, pl.ds((2 - d) * TOK, TOK)],
            send_sem=w_send.at[d - 1],
            recv_sem=w_recv.at[d - 1],
            device_id={"ctx": (c + d) % CTX},
            device_id_type=MESH,
        )

    def wait_cross(column):
        chunk = kv.at[:, pl.ds(0, SUB)]
        pltpu.make_async_copy(chunk, chunk, x_recv.at[column]).wait()

    def onward_copy():
        return pltpu.make_async_remote_copy(
            src_ref=kv.at[:, pl.ds(TOK, TOK)],
            dst_ref=kv.at[:, pl.ds(0, TOK)],
            send_sem=w_send.at[1],
            recv_sem=w_recv.at[1],
            device_id={"ctx": (c + 1) % CTX},
            device_id_type=MESH,
        )

    for d in (1, 2):

        @pl.when(p < PLANE - d)
        def _():
            window_copy(d).start()

    def turn(start):
        for i in range(TOK // TILE):
            at = start + i * TILE
            for w in range(2):
                block = kv[w, at : at + TILE, :].astype(jnp.float32)
                kvt[w, :, at : at + TILE] = block.T.astype(jnp.bfloat16)

    turn(2 * TOK)

    @pl.when((p == 0) & (plane >= 1))
    def _():
        for column in range(8):
            wait_cross(column)
        onward_copy().start()
        for column in range(8, 16):
            wait_cross(column)

    for d in (1, 2):

        @pl.when((p >= 1) & (c >= d))
        def _():
            window_copy(d).wait_recv()

        if d == 2:
            for to in targets[EARLY:]:
                query_copy(to).start()
        turn((2 - d) * TOK)

    lane = lax.broadcasted_iota(jnp.int32, (TILE, LANES), 1) % SUB
    place = lax.broadcasted_iota(jnp.int32, (TILE, LANES), 0)

    def term_copy(part):
        d, start, size = PARTS[part]
        return pltpu.make_async_remote_copy(
            src_ref=tx.at[:, pl.ds(start, size)],
            dst_ref=rx.at[:, pl.ds(start, size)],
            send_sem=t_send.at[part],
            recv_sem=t_recv.at[part],
            device_id={"ctx": (c + CTX - d) % CTX},
            device_id_type=MESH,
        )

    def send_terms(part):
        d, start, size = PARTS[part]
        tx[0, start : start + size] = (acc[0, start : start + size] * SCALING).astype(jnp.bfloat16)
        tx[1, start : start + size] = acc[1, start : start + size].astype(jnp.bfloat16)

        @pl.when(c >= d)
        def _():
            term_copy(part).start()

    early_half = zh < 2

    def unit(i, final):
        a = i // 2
        dz = a + a // 2 - 2 * (a // 3)
        sz, sc = (zh + dz) % 4, (co + i) % 2
        j = sz * 2 + sc

        def arrived():
            pltpu.make_async_copy(qg.at[j], qg.at[j], q_recv.at[j]).wait()

        if final:
            arrived()
        else:
            pl.when(i > 0)(arrived)
        base = pl.multiple_of(sz * TILE, TILE)

        def keys(n):
            return pl.ds(pl.multiple_of(base + n * TILE, TILE), TILE)

        qs = qg[j, :GROUP].reshape(LANES, HD)
        gs = qg[j, GROUP:].reshape(LANES, HD)
        seg_q = segrow[j][0:1]
        causal = place <= lane + sc * SUB

        peak = None
        for n in range(TILES):
            s = dot_nt(kv[0, keys(n), :], qs)
            seg_k = segcol[keys(n), :]
            allowed = jnp.concatenate([seg_k, seg_k], 1) == seg_q
            if n == TILES - 1:
                allowed = allowed & causal
            s = jnp.where(allowed, s, NEGATIVE)
            s_scr[n * TILE : (n + 1) * TILE, :] = s
            here = fold(s, jnp.maximum)
            peak = here if peak is None else jnp.maximum(peak, here)
        peak = jnp.max(peak, axis=0, keepdims=True) * EXP_SCALE

        total = None
        for n in range(TILES):
            p = jnp.exp2(s_scr[n * TILE : (n + 1) * TILE, :] * EXP_SCALE - peak)
            p_scr[n * TILE : (n + 1) * TILE, :] = p.astype(jnp.bfloat16)
            here = fold(p, jnp.add)
            total = here if total is None else total + here
        inverse = 1.0 / jnp.sum(total, axis=0, keepdims=True)

        window = pl.ds(base, WIN)
        attended = dot(kvt[1, :, window], p_scr[...]) * inverse
        gst = gs.astype(jnp.float32).T * inverse
        gst = gst.astype(jnp.bfloat16)
        delta = jnp.sum(gst.astype(jnp.float32) * attended, axis=0, keepdims=True)
        rows = pl.ds(pl.multiple_of(j * SUB, SUB), SUB)

        def store(ref, value):
            value = value.T.astype(jnp.bfloat16)
            for h in range(GROUP):
                ref[rows, h * HD : (h + 1) * HD] = value[h * SUB : (h + 1) * SUB]

        for n in range(TILES):
            p = p_scr[n * TILE : (n + 1) * TILE, :]
            slope = dot(kv[1, keys(n), :], gst)
            e = (p.astype(jnp.float32) * (slope - delta)).astype(jnp.bfloat16)
            e_scr[n * TILE : (n + 1) * TILE, :] = e
            acc[0, keys(n), :] += dot(e, qs)
            acc[1, keys(n), :] += dot_nt(p, gst)
            if final and n == 3:

                @pl.when(jnp.logical_not(early_half))
                def _():
                    send_terms(0)

                send_terms(1)
            if final and n == 7:
                send_terms(2)
        store(out_ref, attended)
        store(dq_ref, dot(kvt[0, :, window], e_scr[...]) * SCALING)

    def one_unit(i, carry):
        unit(i, False)

        @pl.when((i == TP - 3) & early_half)
        def _():
            send_terms(0)

        return carry

    lax.fori_loop(0, TP - 1, one_unit, 0)
    unit(TP - 1, True)

    for part, (d, start, size) in enumerate(PARTS):

        @pl.when(c < CTX - d)
        def _():
            term_copy(part).wait_recv()

        @pl.when(c >= CTX - d)
        def _():
            rx[:, start : start + size] = jnp.zeros((2, size, HD), jnp.bfloat16)

    for w, ref in ((0, dk_ref), (1, dv_ref)):
        own_sum = acc[w, 2 * TOK : 3 * TOK, :]
        if w == 0:
            own_sum = own_sum * SCALING
        far = rx[w, 0:TOK].astype(jnp.float32)
        near = rx[w, TOK : 2 * TOK].astype(jnp.float32)
        ref[...] = (own_sum + near + far).astype(jnp.bfloat16)

    for dz, dc in partners:
        key_copy(partner(dz, dc)).wait_send()
        query_copy(partner(dz, dc)).wait_send()
    @pl.when((p >= 14) & crossing)
    def _():
        for r in range(TP):
            if r != 6:
                relay_copy(r).wait_send()

    @pl.when((p == 15) & crossing)
    def _():
        relay_copy(6).wait_send()

    @pl.when(crossing)
    def _():
        cross_copy(relay).wait_send()

    @pl.when((p == 0) & (plane >= 1))
    def _():
        onward_copy().wait_send()

    for d in (1, 2):

        @pl.when(p < PLANE - d)
        def _():
            window_copy(d).wait_send()

    for part, (d, start, size) in enumerate(PARTS):

        @pl.when(c >= d)
        def _():
            term_copy(part).wait_send()


def hand_over(*refs):
    sources, results, held, come, gone = refs[:4], refs[4:8], refs[8:12], refs[12], refs[13]
    ins = [pltpu.make_async_copy(sources[i], held[i], come.at[i]) for i in range(4)]
    outs = [pltpu.make_async_copy(held[i], results[i], gone.at[i]) for i in range(4)]
    for copy in ins:
        copy.start()
    for copy, onward in zip(ins, outs):
        copy.wait()
        onward.start()
    for onward in outs:
        onward.wait()


def on_device(query, key_states, value_states, grad_out, segment_ids):
    vmem = pl.BlockSpec(memory_space=pltpu.VMEM)
    hbm = pl.BlockSpec(memory_space=pltpu.HBM)
    bf16, f32 = jnp.bfloat16, jnp.float32
    dma = pltpu.SemaphoreType.DMA
    shapes = (
            jax.ShapeDtypeStruct((TOK, GROUP * HD), bf16),
            jax.ShapeDtypeStruct((TOK, GROUP * HD), bf16),
            jax.ShapeDtypeStruct((TOK, HD), bf16),
            jax.ShapeDtypeStruct((TOK, HD), bf16),
    )
    results = pl.pallas_call(
        kernel,
        out_shape=shapes,
        in_specs=[hbm, hbm, hbm, hbm, hbm],
        out_specs=(vmem, vmem, vmem, vmem),
        scratch_shapes=[
            pltpu.VMEM((SUB, QH * HD), bf16),
            pltpu.VMEM((SUB, QH * HD), bf16),
            pltpu.VMEM((SUB, KVH * HD), bf16),
            pltpu.VMEM((SUB, KVH * HD), bf16),
            pltpu.VMEM((TP, 2, SUB, HD), bf16),
            pltpu.VMEM((TP, 2 * GROUP, SUB, HD), bf16),
            pltpu.VMEM((TP, 2 * GROUP, SUB, HD), bf16),
            pltpu.VMEM((2, 3 * TOK, HD), bf16),
            pltpu.VMEM((2, HD, 3 * TOK), bf16),
            pltpu.VMEM((3 * TOK, TILE), f32),
            pltpu.VMEM((TP, 8, LANES), f32),
            pltpu.VMEM((WIN, LANES), f32),
            pltpu.VMEM((WIN, LANES), bf16),
            pltpu.VMEM((WIN, LANES), bf16),
            pltpu.VMEM((2, 3 * TOK, HD), f32),
            pltpu.VMEM((2, 2 * TOK, HD), bf16),
            pltpu.VMEM((2, 2 * TOK, HD), bf16),
        ]
        + [dma((4,))]
        + [dma((TP,))] * 4
        + [dma((2,))] * 2
        + [dma((3,))] * 2
        + [
            pltpu.VMEM((CTX * TOK // TILE, TILE), jnp.int32),
            pltpu.VMEM((2, SUB, HD), bf16),
            dma,
            dma((TP,)),
            dma,
            dma,
            dma((PLANE,)),
        ],
        compiler_params=pltpu.CompilerParams(
            collective_id=0, has_side_effects=True, vmem_limit_bytes=56 * 2**20
        ),
        cost_estimate=pl.CostEstimate(
            flops=2 * 6 * TP * LANES * WIN * HD,
            bytes_accessed=4 * TOK * GROUP * HD * 2,
            transcendentals=TP * LANES * WIN,
        ),
        name="attention",
    )(query, key_states, value_states, grad_out, segment_ids.reshape(-1, TILE))
    whole = pl.BlockSpec(memory_space=pl.ANY)
    return pl.pallas_call(
        hand_over,
        out_shape=shapes,
        in_specs=[whole] * 4,
        out_specs=(whole,) * 4,
        scratch_shapes=[pltpu.VMEM(shape.shape, shape.dtype) for shape in shapes]
        + [dma((4,)), dma((4,))],
        compiler_params=pltpu.CompilerParams(vmem_limit_bytes=56 * 2**20),
        name="hand_over",
    )(*results)


def solution(mesh):
    in_specs = (
        P(("ctx", "tp"), None),
        P(("ctx", "tp"), None),
        P(("ctx", "tp"), None),
        P(("ctx", "tp"), None),
        P(),
    )
    out_specs = (P("ctx", "tp"), P("ctx", "tp"), P("ctx", "tp"), P("ctx", "tp"))
    return jax.shard_map(
        on_device, mesh=mesh, in_specs=in_specs, out_specs=out_specs, check_vma=False
    )
```

```python
import math

import jax
import jax.numpy as jnp
from jax import lax
from jax.experimental import pallas as pl
from jax.experimental.pallas import tpu as pltpu
from jax.sharding import PartitionSpec as P

QH = 32
KVH = 8
HD = 128
TOK = 512
SUB = 64
GROUP = QH // KVH
CTX = 64
PLANE = 16
PLANES = CTX // PLANE
EARLY = 3
TP = 8
HALF = SUB * GROUP
LANES = 2 * HALF
UNITS = TP // 2
WIN = 1152
TILE = 128
TILES = WIN // TILE
NEGATIVE = -1e30
MESH = pl.DeviceIdType.MESH
SCALING = HD**-0.5
EXP_SCALE = SCALING * math.log2(math.e)

PARTS = ((2, 0, 256), (2, 256, 256), (1, 512, 256), (1, 768, 256))

NT = (((1,), (1,)), ((), ()))


def dot(a, b):
    return jnp.dot(a, b, preferred_element_type=jnp.float32)


def dot_nt(a, b):
    return lax.dot_general(a, b, NT, preferred_element_type=jnp.float32)


def fold(x, op):
    parts = [x[i * 8 : (i + 1) * 8] for i in range(x.shape[0] // 8)]
    while len(parts) > 1:
        parts = [op(parts[i], parts[i + 1]) for i in range(0, len(parts), 2)]
    return parts[0]


def kernel(
    q_in,
    k_in,
    v_in,
    g_in,
    seg_in,
    out_ref,
    dq_ref,
    dk_ref,
    dv_ref,
    q_vm,
    g_vm,
    k_vm,
    v_vm,
    kv_out,
    qg_out,
    qg,
    kv,
    kvt,
    segcol,
    segrow,
    s_scr,
    p_scr,
    e_scr,
    gst_scr,
    acc,
    tx,
    rx,
    load_sem,
    q_send,
    q_recv,
    k_send,
    k_recv,
    w_send,
    w_recv,
    t_send,
    t_recv,
    seg,
    relay,
    seg_sem,
    r_send,
    r_recv,
    x_send,
    x_recv,
):
    c = lax.axis_index("ctx")
    t = lax.axis_index("tp")
    zh, co = t // 2, t % 2
    plane, p = c // PLANE, c % PLANE

    seg_copy = pltpu.make_async_copy(seg_in, seg, seg_sem)
    seg_copy.start()
    loads = [
        pltpu.make_async_copy(k_in, k_vm, load_sem.at[0]),
        pltpu.make_async_copy(v_in, v_vm, load_sem.at[1]),
        pltpu.make_async_copy(q_in, q_vm, load_sem.at[2]),
        pltpu.make_async_copy(g_in, g_vm, load_sem.at[3]),
    ]
    for load in loads:
        load.start()

    barrier = pltpu.get_barrier_semaphore()
    for d in range(1, TP):
        pl.semaphore_signal(barrier, inc=1, device_id={"tp": (t + d) % TP}, device_id_type=MESH)
    for d in (1, 2, CTX - 1, CTX - 2):
        pl.semaphore_signal(barrier, inc=1, device_id={"ctx": (c + d) % CTX}, device_id_type=MESH)

    crossing = plane < PLANES - 1

    def greet(block, to=t):
        pl.semaphore_signal(
            barrier, inc=1, device_id={"ctx": block, "tp": to}, device_id_type=MESH
        )

    first = plane * PLANE

    @pl.when(p < 8)
    def _():
        greet(first + 15)

    @pl.when((p >= 8) & (p != 14))
    def _():
        greet(first + 14)

    @pl.when(p == 15)
    def _():
        for r in range(TP):
            greet(first + r)

    @pl.when(p == 14)
    def _():
        for r in range(TP):
            if r != 6:
                greet(first + 8 + r)

    @pl.when((p == 0) & (plane >= 1))
    def _():
        for r in range(TP):
            greet(first - PLANE + t, r)
            greet(first - PLANE + 8 + t, r)

    arrivals = (
        TP - 1 + 4 + jnp.where(p < 14, 1, jnp.where(p == 14, 7, 9)) + jnp.where(crossing, 1, 0)
    )

    def own_rows(j):
        return pl.ds(pl.multiple_of(2 * TOK + j * SUB, SUB), SUB)

    for load in loads:
        load.wait()
    for j in range(TP):
        kv_out[j, 0] = k_vm[:, j * HD : (j + 1) * HD]
        kv_out[j, 1] = v_vm[:, j * HD : (j + 1) * HD]
    for j in range(TP):
        for h in range(GROUP):
            at = (j * GROUP + h) * HD
            qg_out[j, h] = q_vm[:, at : at + HD]
            qg_out[j, GROUP + h] = g_vm[:, at : at + HD]

    @pl.when(c < 1)
    def _():
        kv[:, TOK : 2 * TOK] = jnp.zeros((2, TOK, HD), jnp.bfloat16)

    @pl.when(c < 2)
    def _():
        kv[:, 0:TOK] = jnp.zeros((2, TOK, HD), jnp.bfloat16)

    kv[:, own_rows(t), :] = kv_out[t]
    qg[t] = qg_out[t]
    acc[...] = jnp.zeros_like(acc)

    seg_copy.wait()
    for block in range(3):
        at = jnp.maximum(c - 2 + block, 0)
        rows = seg[pl.ds(pl.multiple_of(at * 4, 4), 4), :].astype(jnp.float32)
        rows = jnp.where(c - 2 + block >= 0, rows, -1.0)
        for i in range(4):
            wide_row = jnp.broadcast_to(rows[i : i + 1], (TILE, TILE))
            start = block * TOK + i * TILE
            segcol[start : start + TILE, :] = wide_row.T
    own = seg[pl.ds(pl.multiple_of(c * 4, 4), 4), :].astype(jnp.float32)
    low_lane = lax.broadcasted_iota(jnp.int32, (8, TILE), 1) < SUB
    for i in range(4):
        row = jnp.broadcast_to(own[i : i + 1], (8, TILE))
        turned = pltpu.roll(row, SUB, 1)
        low = jnp.where(low_lane, row, turned)
        high = jnp.where(low_lane, turned, row)
        segrow[2 * i] = jnp.concatenate([low, low], 1)
        segrow[2 * i + 1] = jnp.concatenate([high, high], 1)

    pl.semaphore_wait(barrier, arrivals)

    def partner(dz, dc):
        return ((zh + dz) % 4) * 2 + (co + dc) % 2

    partners = [(1, 0), (3, 0), (1, 1), (3, 1), (2, 0), (2, 1), (0, 1)]
    to_1, to_2, to_3 = (zh + 1) % 4, (zh + 3) % 4, (zh + 2) % 4
    targets = [zh * 2 + 1 - co, to_1 * 2 + co, to_2 * 2 + co]
    targets += [to_1 * 2 + 1 - co, to_2 * 2 + 1 - co, to_3 * 2 + co, to_3 * 2 + 1 - co]

    def exchange(src, dst, send, recv, to):
        return pltpu.make_async_remote_copy(
            src_ref=src,
            dst_ref=dst,
            send_sem=send.at[to],
            recv_sem=recv.at[t],
            device_id={"tp": to},
            device_id_type=MESH,
        )

    def key_copy(to):
        return exchange(kv_out.at[to], kv.at[:, own_rows(t)], k_send, k_recv, to)

    def query_copy(to):
        return exchange(qg_out.at[to], qg.at[t], q_send, q_recv, to)

    def relay_copy(r):
        return pltpu.make_async_remote_copy(
            src_ref=kv_out.at[r],
            dst_ref=relay,
            send_sem=r_send.at[r],
            recv_sem=r_recv,
            device_id={"ctx": first + r + 8 * (15 - p)},
            device_id_type=MESH,
        )

    def cross_copy(src):
        at = jnp.where(p < 8, TOK, 0) + t * SUB
        return pltpu.make_async_remote_copy(
            src_ref=src,
            dst_ref=kv.at[:, pl.ds(pl.multiple_of(at, SUB), SUB)],
            send_sem=x_send,
            recv_sem=x_recv.at[jnp.where(p < 8, 0, 8) + t],
            device_id={"ctx": (plane + 1) % PLANES * PLANE, "tp": p % 8},
            device_id_type=MESH,
        )

    @pl.when((p == 15) & crossing)
    def _():
        for r in range(TP):
            relay_copy(r).start()

    @pl.when((p == 14) & crossing)
    def _():
        for r in range(TP):
            if r != 6:
                relay_copy(r).start()
        cross_copy(kv_out.at[6]).start()

    for dz, dc in partners:
        key_copy(partner(dz, dc)).start()

    @pl.when((p != 14) & crossing)
    def _():
        pltpu.make_async_copy(relay, relay, r_recv).wait()
        cross_copy(relay).start()

    for to in targets[:EARLY]:
        query_copy(to).start()

    def window_copy(d, j):
        return pltpu.make_async_remote_copy(
            src_ref=kv.at[:, own_rows(j)],
            dst_ref=kv.at[:, pl.ds(pl.multiple_of((2 - d) * TOK + j * SUB, SUB), SUB)],
            send_sem=w_send.at[d - 1],
            recv_sem=w_recv.at[d - 1],
            device_id={"ctx": (c + d) % CTX},
            device_id_type=MESH,
        )

    def wait_window(sem):
        pltpu.make_async_copy(kv.at[:, pl.ds(0, TOK)], kv.at[:, pl.ds(0, TOK)], sem).wait()

    def send_window(j):
        for d in (1, 2):

            @pl.when(p < PLANE - d)
            def _():
                window_copy(d, j).start()

    send_window(t)
    for dz, dc in [(0, 1)] + partners[:-1]:
        j = partner(dz, dc)
        rows = kv.at[:, own_rows(j)]
        pltpu.make_async_copy(rows, rows, k_recv.at[j]).wait()
        send_window(j)

    def wait_cross(column):
        chunk = kv.at[:, pl.ds(0, SUB)]
        pltpu.make_async_copy(chunk, chunk, x_recv.at[column]).wait()

    def onward_copy():
        return pltpu.make_async_remote_copy(
            src_ref=kv.at[:, pl.ds(TOK, TOK)],
            dst_ref=kv.at[:, pl.ds(0, TOK)],
            send_sem=w_send.at[2],
            recv_sem=w_recv.at[1],
            device_id={"ctx": (c + 1) % CTX},
            device_id_type=MESH,
        )

    def turn(start):
        for i in range(TOK // TILE):
            at = start + i * TILE
            for w in range(2):
                block = kv[w, at : at + TILE, :].astype(jnp.float32)
                kvt[w, :, at : at + TILE] = block.T.astype(jnp.bfloat16)

    turn(2 * TOK)

    @pl.when((p == 0) & (plane >= 1))
    def _():
        for column in range(8):
            wait_cross(column)
        onward_copy().start()
        for column in range(8, 16):
            wait_cross(column)

    for d in (1, 2):

        @pl.when((p >= 1) & (c >= d))
        def _():
            wait_window(w_recv.at[d - 1])

        if d == 2:
            for to in targets[EARLY:]:
                query_copy(to).start()
        turn((2 - d) * TOK)

    lane = lax.broadcasted_iota(jnp.int32, (TILE, HALF), 1) % SUB
    place = lax.broadcasted_iota(jnp.int32, (TILE, HALF), 0)

    def term_copy(part):
        d, start, size = PARTS[part]
        return pltpu.make_async_remote_copy(
            src_ref=tx.at[:, pl.ds(start, size)],
            dst_ref=rx.at[:, pl.ds(start, size)],
            send_sem=t_send.at[part],
            recv_sem=t_recv.at[part],
            device_id={"ctx": (c + CTX - d) % CTX},
            device_id_type=MESH,
        )

    def send_terms(part):
        d, start, size = PARTS[part]
        tx[0, start : start + size] = (acc[0, start : start + size] * SCALING).astype(jnp.bfloat16)
        tx[1, start : start + size] = acc[1, start : start + size].astype(jnp.bfloat16)

        @pl.when(c >= d)
        def _():
            term_copy(part).start()

    early_half = zh < 2

    def unit(i, final):
        dz = i + i // 2 - 2 * (i // 3)
        sz = (zh + dz) % 4

        def arrived(j):
            pltpu.make_async_copy(qg.at[j], qg.at[j], q_recv.at[j]).wait()

        if final:
            arrived(sz * 2 + co)
        else:
            pl.when(i > 0)(lambda: arrived(sz * 2 + co))
        arrived(sz * 2 + 1 - co)
        base = pl.multiple_of(sz * TILE, TILE)
        window = pl.ds(base, WIN)
        halves = [slice(0, HALF), slice(HALF, LANES)]

        def keys(n):
            return pl.ds(pl.multiple_of(base + n * TILE, TILE), TILE)

        def tile(n):
            return slice(n * TILE, (n + 1) * TILE)

        both = pl.ds(sz * 2, 2)
        qs = qg[both, :GROUP].reshape(LANES, HD)
        gs = qg[both, GROUP:].reshape(LANES, HD)

        terms = []
        for half, at in enumerate(halves):
            seg_q = segrow[sz * 2 + half][0:1]
            causal = place <= lane + half * SUB
            peak = None
            for n in range(TILES):
                s = dot_nt(kv[0, keys(n), :], qs[at])
                seg_k = segcol[keys(n), :]
                allowed = jnp.concatenate([seg_k, seg_k], 1) == seg_q
                if n == TILES - 1:
                    allowed = allowed & causal
                s = jnp.where(allowed, s, NEGATIVE)
                s_scr[tile(n), at] = s
                here = fold(s, jnp.maximum)
                peak = here if peak is None else jnp.maximum(peak, here)
            peak = jnp.max(peak, axis=0, keepdims=True) * EXP_SCALE

            total = None
            for n in range(TILES):
                p = jnp.exp2(s_scr[tile(n), at] * EXP_SCALE - peak)
                p_scr[tile(n), at] = p.astype(jnp.bfloat16)
                here = fold(p, jnp.add)
                total = here if total is None else total + here
            inverse = 1.0 / jnp.sum(total, axis=0, keepdims=True)

            attended = dot(kvt[1, :, window], p_scr[:, at]) * inverse
            gst = (gs[at].astype(jnp.float32).T * inverse).astype(jnp.bfloat16)
            delta = jnp.sum(gst.astype(jnp.float32) * attended, axis=0, keepdims=True)
            gst_scr[:, at] = gst
            terms.append((attended, gst, delta))

        def store(ref, half, value):
            value = value.T.astype(jnp.bfloat16)
            rows = pl.ds(pl.multiple_of(base + half * SUB, SUB), SUB)
            for h in range(GROUP):
                ref[rows, h * HD : (h + 1) * HD] = value[h * SUB : (h + 1) * SUB]

        for n in range(TILES):
            for half, at in enumerate(halves):
                attended, gst, delta = terms[half]
                slope = dot(kv[1, keys(n), :], gst)
                p = p_scr[tile(n), at].astype(jnp.float32)
                e_scr[tile(n), at] = (p * (slope - delta)).astype(jnp.bfloat16)
            acc[0, keys(n), :] += dot(e_scr[tile(n), :], qs)
            acc[1, keys(n), :] += dot_nt(p_scr[tile(n), :], gst_scr[...])
            if final and n == 1:

                @pl.when(jnp.logical_not(early_half))
                def _():
                    send_terms(0)

            if final and n in (3, 5, 7):
                send_terms(n // 2)
        for half, at in enumerate(halves):
            store(out_ref, half, terms[half][0])
            store(dq_ref, half, dot(kvt[0, :, window], e_scr[:, at]) * SCALING)

    def one_unit(i, carry):
        unit(i, False)
        return carry

    lax.fori_loop(0, UNITS - 1, one_unit, 0)

    @pl.when(early_half)
    def _():
        send_terms(0)

    unit(UNITS - 1, True)

    for part, (d, start, size) in enumerate(PARTS):

        @pl.when(c < CTX - d)
        def _():
            term_copy(part).wait_recv()

        @pl.when(c >= CTX - d)
        def _():
            rx[:, start : start + size] = jnp.zeros((2, size, HD), jnp.bfloat16)

    for w, ref in ((0, dk_ref), (1, dv_ref)):
        own_sum = acc[w, 2 * TOK : 3 * TOK, :]
        if w == 0:
            own_sum = own_sum * SCALING
        far = rx[w, 0:TOK].astype(jnp.float32)
        near = rx[w, TOK : 2 * TOK].astype(jnp.float32)
        ref[...] = (own_sum + near + far).astype(jnp.bfloat16)

    for dz, dc in partners:
        key_copy(partner(dz, dc)).wait_send()
        query_copy(partner(dz, dc)).wait_send()
    @pl.when((p >= 14) & crossing)
    def _():
        for r in range(TP):
            if r != 6:
                relay_copy(r).wait_send()

    @pl.when((p == 15) & crossing)
    def _():
        relay_copy(6).wait_send()

    @pl.when(crossing)
    def _():
        cross_copy(relay).wait_send()

    @pl.when((p == 0) & (plane >= 1))
    def _():
        onward_copy().wait_send()

    for d in (1, 2):

        @pl.when(p < PLANE - d)
        def _():
            wait_window(w_send.at[d - 1])

    for part, (d, start, size) in enumerate(PARTS):

        @pl.when(c >= d)
        def _():
            term_copy(part).wait_send()


def hand_over(*refs):
    sources, results, held, come, gone = refs[:4], refs[4:8], refs[8:12], refs[12], refs[13]
    ins = [pltpu.make_async_copy(sources[i], held[i], come.at[i]) for i in range(4)]
    outs = [pltpu.make_async_copy(held[i], results[i], gone.at[i]) for i in range(4)]
    for copy in ins:
        copy.start()
    for copy, onward in zip(ins, outs):
        copy.wait()
        onward.start()
    for onward in outs:
        onward.wait()


def on_device(query, key_states, value_states, grad_out, segment_ids):
    vmem = pl.BlockSpec(memory_space=pltpu.VMEM)
    hbm = pl.BlockSpec(memory_space=pltpu.HBM)
    bf16, f32 = jnp.bfloat16, jnp.float32
    dma = pltpu.SemaphoreType.DMA
    shapes = (
            jax.ShapeDtypeStruct((TOK, GROUP * HD), bf16),
            jax.ShapeDtypeStruct((TOK, GROUP * HD), bf16),
            jax.ShapeDtypeStruct((TOK, HD), bf16),
            jax.ShapeDtypeStruct((TOK, HD), bf16),
    )
    results = pl.pallas_call(
        kernel,
        out_shape=shapes,
        in_specs=[hbm, hbm, hbm, hbm, hbm],
        out_specs=(vmem, vmem, vmem, vmem),
        scratch_shapes=[
            pltpu.VMEM((SUB, QH * HD), bf16),
            pltpu.VMEM((SUB, QH * HD), bf16),
            pltpu.VMEM((SUB, KVH * HD), bf16),
            pltpu.VMEM((SUB, KVH * HD), bf16),
            pltpu.VMEM((TP, 2, SUB, HD), bf16),
            pltpu.VMEM((TP, 2 * GROUP, SUB, HD), bf16),
            pltpu.VMEM((TP, 2 * GROUP, SUB, HD), bf16),
            pltpu.VMEM((2, 3 * TOK, HD), bf16),
            pltpu.VMEM((2, HD, 3 * TOK), bf16),
            pltpu.VMEM((3 * TOK, TILE), f32),
            pltpu.VMEM((TP, 8, HALF), f32),
            pltpu.VMEM((WIN, LANES), f32),
            pltpu.VMEM((WIN, LANES), bf16),
            pltpu.VMEM((WIN, LANES), bf16),
            pltpu.VMEM((HD, LANES), bf16),
            pltpu.VMEM((2, 3 * TOK, HD), f32),
            pltpu.VMEM((2, 2 * TOK, HD), bf16),
            pltpu.VMEM((2, 2 * TOK, HD), bf16),
        ]
        + [dma((4,))]
        + [dma((TP,))] * 4
        + [dma((3,)), dma((2,)), dma((4,)), dma((4,))]
        + [
            pltpu.VMEM((CTX * TOK // TILE, TILE), jnp.int32),
            pltpu.VMEM((2, SUB, HD), bf16),
            dma,
            dma((TP,)),
            dma,
            dma,
            dma((PLANE,)),
        ],
        compiler_params=pltpu.CompilerParams(
            collective_id=0, has_side_effects=True, vmem_limit_bytes=56 * 2**20
        ),
        cost_estimate=pl.CostEstimate(
            flops=2 * 6 * UNITS * LANES * WIN * HD,
            bytes_accessed=4 * TOK * GROUP * HD * 2,
            transcendentals=UNITS * LANES * WIN,
        ),
        name="attention",
    )(query, key_states, value_states, grad_out, segment_ids.reshape(-1, TILE))
    whole = pl.BlockSpec(memory_space=pl.ANY)
    return pl.pallas_call(
        hand_over,
        out_shape=shapes,
        in_specs=[whole] * 4,
        out_specs=(whole,) * 4,
        scratch_shapes=[pltpu.VMEM(shape.shape, shape.dtype) for shape in shapes]
        + [dma((4,)), dma((4,))],
        compiler_params=pltpu.CompilerParams(vmem_limit_bytes=56 * 2**20),
        name="hand_over",
    )(*results)


def solution(mesh):
    in_specs = (
        P(("ctx", "tp"), None),
        P(("ctx", "tp"), None),
        P(("ctx", "tp"), None),
        P(("ctx", "tp"), None),
        P(),
    )
    out_specs = (P("ctx", "tp"), P("ctx", "tp"), P("ctx", "tp"), P("ctx", "tp"))
    return jax.shard_map(
        on_device, mesh=mesh, in_specs=in_specs, out_specs=out_specs, check_vma=False
    )
```

```python
import math

import jax
import jax.numpy as jnp
from jax import lax
from jax.experimental import pallas as pl
from jax.experimental.pallas import tpu as pltpu
from jax.sharding import PartitionSpec as P

QH = 32
KVH = 8
HD = 128
TOK = 512
SUB = 64
GROUP = QH // KVH
CTX = 64
PLANE = 16
PLANES = CTX // PLANE
EARLY = 5
TP = 8
HALF = SUB * GROUP
LANES = 2 * HALF
UNITS = TP // 2
WIN = 1152
TILE = 128
TILES = WIN // TILE
NEGATIVE = -1e30
MESH = pl.DeviceIdType.MESH
SCALING = HD**-0.5
EXP_SCALE = SCALING * math.log2(math.e)

PARTS = ((2, 0, 256), (2, 256, 256), (1, 512, 256), (1, 768, 256))

NT = (((1,), (1,)), ((), ()))


def dot(a, b):
    return jnp.dot(a, b, preferred_element_type=jnp.float32)


def dot_nt(a, b):
    return lax.dot_general(a, b, NT, preferred_element_type=jnp.float32)


def fold(x, op):
    parts = [x[i * 8 : (i + 1) * 8] for i in range(x.shape[0] // 8)]
    while len(parts) > 1:
        parts = [op(parts[i], parts[i + 1]) for i in range(0, len(parts), 2)]
    return parts[0]


def kernel(
    q_in,
    k_in,
    v_in,
    g_in,
    seg_in,
    out_ref,
    dq_ref,
    dk_ref,
    dv_ref,
    q_vm,
    g_vm,
    k_vm,
    v_vm,
    kv_out,
    qg_out,
    qg,
    kv,
    kvt,
    segcol,
    segrow,
    s_scr,
    p_scr,
    e_scr,
    gst_scr,
    acc,
    tx,
    rx,
    load_sem,
    q_send,
    q_recv,
    k_send,
    k_recv,
    w_send,
    w_recv,
    t_send,
    t_recv,
    seg,
    relay,
    seg_sem,
    r_send,
    r_recv,
    x_send,
    x_recv,
):
    c = lax.axis_index("ctx")
    t = lax.axis_index("tp")
    zh, co = t // 2, t % 2
    plane, p = c // PLANE, c % PLANE

    seg_copy = pltpu.make_async_copy(seg_in, seg, seg_sem)
    seg_copy.start()
    loads = [
        pltpu.make_async_copy(k_in, k_vm, load_sem.at[0]),
        pltpu.make_async_copy(v_in, v_vm, load_sem.at[1]),
        pltpu.make_async_copy(q_in, q_vm, load_sem.at[2]),
        pltpu.make_async_copy(g_in, g_vm, load_sem.at[3]),
    ]
    for load in loads:
        load.start()

    barrier = pltpu.get_barrier_semaphore()
    for d in range(1, TP):
        pl.semaphore_signal(barrier, inc=1, device_id={"tp": (t + d) % TP}, device_id_type=MESH)
    for d in (1, 2, CTX - 1, CTX - 2):
        pl.semaphore_signal(barrier, inc=1, device_id={"ctx": (c + d) % CTX}, device_id_type=MESH)

    crossing = plane < PLANES - 1

    def greet(block, to=t):
        pl.semaphore_signal(
            barrier, inc=1, device_id={"ctx": block, "tp": to}, device_id_type=MESH
        )

    first = plane * PLANE

    @pl.when(p < 8)
    def _():
        greet(first + 15)

    @pl.when((p >= 8) & (p != 14))
    def _():
        greet(first + 14)

    @pl.when(p == 15)
    def _():
        for r in range(TP):
            greet(first + r)

    @pl.when(p == 14)
    def _():
        for r in range(TP):
            if r != 6:
                greet(first + 8 + r)

    @pl.when((p == 0) & (plane >= 1))
    def _():
        for r in range(TP):
            greet(first - PLANE + t, r)
            greet(first - PLANE + 8 + t, r)

    arrivals = (
        TP - 1 + 4 + jnp.where(p < 14, 1, jnp.where(p == 14, 7, 9)) + jnp.where(crossing, 1, 0)
    )

    def own_rows(j):
        return pl.ds(pl.multiple_of(2 * TOK + j * SUB, SUB), SUB)

    for load in loads:
        load.wait()
    for j in range(TP):
        kv_out[j, 0] = k_vm[:, j * HD : (j + 1) * HD]
        kv_out[j, 1] = v_vm[:, j * HD : (j + 1) * HD]
    for j in range(TP):
        for h in range(GROUP):
            at = (j * GROUP + h) * HD
            qg_out[j, h] = q_vm[:, at : at + HD]
            qg_out[j, GROUP + h] = g_vm[:, at : at + HD]

    kv[:, own_rows(t), :] = kv_out[t]
    qg[t] = qg_out[t]

    pl.semaphore_wait(barrier, arrivals)

    def partner(dz, dc):
        return ((zh + dz) % 4) * 2 + (co + dc) % 2

    partners = [(1, 0), (3, 0), (1, 1), (3, 1), (2, 0), (2, 1), (0, 1)]
    across, below, above = (zh + 2) % 4, (zh + 3) % 4, (zh + 1) % 4
    targets = [zh * 2 + 1 - co, across * 2 + co, across * 2 + 1 - co]
    targets += [below * 2 + co, above * 2 + co, below * 2 + 1 - co, above * 2 + 1 - co]

    def exchange(src, dst, send, recv, to):
        return pltpu.make_async_remote_copy(
            src_ref=src,
            dst_ref=dst,
            send_sem=send.at[to],
            recv_sem=recv.at[t],
            device_id={"tp": to},
            device_id_type=MESH,
        )

    def key_copy(to):
        return exchange(kv_out.at[to], kv.at[:, own_rows(t)], k_send, k_recv, to)

    def query_copy(to):
        return exchange(qg_out.at[to], qg.at[t], q_send, q_recv, to)

    def relay_copy(r):
        return pltpu.make_async_remote_copy(
            src_ref=kv_out.at[r],
            dst_ref=relay,
            send_sem=r_send.at[r],
            recv_sem=r_recv,
            device_id={"ctx": first + r + 8 * (15 - p)},
            device_id_type=MESH,
        )

    def cross_copy(src):
        at = jnp.where(p < 8, TOK, 0) + t * SUB
        return pltpu.make_async_remote_copy(
            src_ref=src,
            dst_ref=kv.at[:, pl.ds(pl.multiple_of(at, SUB), SUB)],
            send_sem=x_send,
            recv_sem=x_recv.at[jnp.where(p < 8, 0, 8) + t],
            device_id={"ctx": (plane + 1) % PLANES * PLANE, "tp": p % 8},
            device_id_type=MESH,
        )

    @pl.when((p == 15) & crossing)
    def _():
        for r in range(TP):
            relay_copy(r).start()

    @pl.when((p == 14) & crossing)
    def _():
        for r in range(TP):
            if r != 6:
                relay_copy(r).start()
        cross_copy(kv_out.at[6]).start()

    for dz, dc in partners:
        key_copy(partner(dz, dc)).start()

    @pl.when((p != 14) & crossing)
    def _():
        pltpu.make_async_copy(relay, relay, r_recv).wait()
        cross_copy(relay).start()

    for to in targets[:EARLY]:
        query_copy(to).start()

    @pl.when(c < 1)
    def _():
        kv[:, TOK : 2 * TOK] = jnp.zeros((2, TOK, HD), jnp.bfloat16)

    @pl.when(c < 2)
    def _():
        kv[:, 0:TOK] = jnp.zeros((2, TOK, HD), jnp.bfloat16)

    acc[...] = jnp.zeros_like(acc)

    seg_copy.wait()
    for block in range(3):
        at = jnp.maximum(c - 2 + block, 0)
        rows = seg[pl.ds(pl.multiple_of(at * 4, 4), 4), :].astype(jnp.float32)
        rows = jnp.where(c - 2 + block >= 0, rows, -1.0)
        for i in range(4):
            wide_row = jnp.broadcast_to(rows[i : i + 1], (TILE, TILE))
            start = block * TOK + i * TILE
            segcol[start : start + TILE, :] = wide_row.T
    own = seg[pl.ds(pl.multiple_of(c * 4, 4), 4), :].astype(jnp.float32)
    low_lane = lax.broadcasted_iota(jnp.int32, (8, TILE), 1) < SUB
    for i in range(4):
        row = jnp.broadcast_to(own[i : i + 1], (8, TILE))
        turned = pltpu.roll(row, SUB, 1)
        low = jnp.where(low_lane, row, turned)
        high = jnp.where(low_lane, turned, row)
        segrow[2 * i] = jnp.concatenate([low, low], 1)
        segrow[2 * i + 1] = jnp.concatenate([high, high], 1)

    def window_copy(d, j):
        return pltpu.make_async_remote_copy(
            src_ref=kv.at[:, own_rows(j)],
            dst_ref=kv.at[:, pl.ds(pl.multiple_of((2 - d) * TOK + j * SUB, SUB), SUB)],
            send_sem=w_send.at[d - 1],
            recv_sem=w_recv.at[d - 1],
            device_id={"ctx": (c + d) % CTX},
            device_id_type=MESH,
        )

    def wait_window(sem):
        pltpu.make_async_copy(kv.at[:, pl.ds(0, TOK)], kv.at[:, pl.ds(0, TOK)], sem).wait()

    def send_window(j):
        for d in (1, 2):

            @pl.when(p < PLANE - d)
            def _():
                window_copy(d, j).start()

    send_window(t)
    for dz, dc in [(0, 1)] + partners[:-1]:
        j = partner(dz, dc)
        rows = kv.at[:, own_rows(j)]
        pltpu.make_async_copy(rows, rows, k_recv.at[j]).wait()
        send_window(j)

    def wait_cross(column):
        chunk = kv.at[:, pl.ds(0, SUB)]
        pltpu.make_async_copy(chunk, chunk, x_recv.at[column]).wait()

    def onward_copy():
        return pltpu.make_async_remote_copy(
            src_ref=kv.at[:, pl.ds(TOK, TOK)],
            dst_ref=kv.at[:, pl.ds(0, TOK)],
            send_sem=w_send.at[2],
            recv_sem=w_recv.at[1],
            device_id={"ctx": (c + 1) % CTX},
            device_id_type=MESH,
        )

    def turn(start):
        for i in range(TOK // TILE):
            at = start + i * TILE
            for w in range(2):
                block = kv[w, at : at + TILE, :].astype(jnp.float32)
                kvt[w, :, at : at + TILE] = block.T.astype(jnp.bfloat16)

    turn(2 * TOK)

    @pl.when((p == 0) & (plane >= 1))
    def _():
        for column in range(8):
            wait_cross(column)
        onward_copy().start()
        for column in range(8, 16):
            wait_cross(column)

    for d in (1, 2):

        @pl.when((p >= 1) & (c >= d))
        def _():
            wait_window(w_recv.at[d - 1])

        if d == 2:
            for to in targets[EARLY:]:
                query_copy(to).start()
        turn((2 - d) * TOK)

    lane = lax.broadcasted_iota(jnp.int32, (TILE, HALF), 1) % SUB
    place = lax.broadcasted_iota(jnp.int32, (TILE, HALF), 0)

    def term_copy(part):
        d, start, size = PARTS[part]
        return pltpu.make_async_remote_copy(
            src_ref=tx.at[:, pl.ds(start, size)],
            dst_ref=rx.at[:, pl.ds(start, size)],
            send_sem=t_send.at[part],
            recv_sem=t_recv.at[part],
            device_id={"ctx": (c + CTX - d) % CTX},
            device_id_type=MESH,
        )

    def send_terms(part):
        d, start, size = PARTS[part]
        tx[0, start : start + size] = (acc[0, start : start + size] * SCALING).astype(jnp.bfloat16)
        tx[1, start : start + size] = acc[1, start : start + size].astype(jnp.bfloat16)

        @pl.when(c >= d)
        def _():
            term_copy(part).start()

    outer = (zh == 0) | (zh == 3)

    def unit(i, final):
        dz = jnp.where(i < 2, i * 2, jnp.where((i == 2) == outer, 1, 3))
        sz = (zh + dz) % 4

        def arrived(j):
            pltpu.make_async_copy(qg.at[j], qg.at[j], q_recv.at[j]).wait()

        if final:
            arrived(sz * 2 + co)
        else:
            pl.when(i > 0)(lambda: arrived(sz * 2 + co))
        arrived(sz * 2 + 1 - co)
        base = pl.multiple_of(sz * TILE, TILE)
        window = pl.ds(base, WIN)
        halves = [slice(0, HALF), slice(HALF, LANES)]

        def keys(n):
            return pl.ds(pl.multiple_of(base + n * TILE, TILE), TILE)

        def tile(n):
            return slice(n * TILE, (n + 1) * TILE)

        both = pl.ds(sz * 2, 2)
        qs = qg[both, :GROUP].reshape(LANES, HD)
        gs = qg[both, GROUP:].reshape(LANES, HD)

        terms = []
        for half, at in enumerate(halves):
            seg_q = segrow[sz * 2 + half][0:1]
            causal = place <= lane + half * SUB
            peak = None
            for n in range(TILES):
                s = dot_nt(kv[0, keys(n), :], qs[at])
                seg_k = segcol[keys(n), :]
                allowed = jnp.concatenate([seg_k, seg_k], 1) == seg_q
                if n == TILES - 1:
                    allowed = allowed & causal
                s = jnp.where(allowed, s, NEGATIVE)
                s_scr[tile(n), at] = s
                here = fold(s, jnp.maximum)
                peak = here if peak is None else jnp.maximum(peak, here)
            peak = jnp.max(peak, axis=0, keepdims=True) * EXP_SCALE

            total = None
            for n in range(TILES):
                p = jnp.exp2(s_scr[tile(n), at] * EXP_SCALE - peak)
                p_scr[tile(n), at] = p.astype(jnp.bfloat16)
                here = fold(p, jnp.add)
                total = here if total is None else total + here
            inverse = 1.0 / jnp.sum(total, axis=0, keepdims=True)

            attended = dot(kvt[1, :, window], p_scr[:, at]) * inverse
            gst = (gs[at].astype(jnp.float32).T * inverse).astype(jnp.bfloat16)
            delta = jnp.sum(gst.astype(jnp.float32) * attended, axis=0, keepdims=True)
            gst_scr[:, at] = gst
            terms.append((attended, gst, delta))

        def store(ref, half, value):
            value = value.T.astype(jnp.bfloat16)
            rows = pl.ds(pl.multiple_of(base + half * SUB, SUB), SUB)
            for h in range(GROUP):
                ref[rows, h * HD : (h + 1) * HD] = value[h * SUB : (h + 1) * SUB]

        for n in range(TILES):
            for half, at in enumerate(halves):
                attended, gst, delta = terms[half]
                slope = dot(kv[1, keys(n), :], gst)
                p = p_scr[tile(n), at].astype(jnp.float32)
                e_scr[tile(n), at] = (p * (slope - delta)).astype(jnp.bfloat16)
            acc[0, keys(n), :] += dot(e_scr[tile(n), :], qs)
            acc[1, keys(n), :] += dot_nt(p_scr[tile(n), :], gst_scr[...])
            if final and n in (3, 5, 7):
                send_terms(n // 2)
        for half, at in enumerate(halves):
            store(out_ref, half, terms[half][0])
            store(dq_ref, half, dot(kvt[0, :, window], e_scr[:, at]) * SCALING)

    def one_unit(i, carry):
        unit(i, False)
        return carry

    lax.fori_loop(0, UNITS - 1, one_unit, 0)

    send_terms(0)
    unit(UNITS - 1, True)

    for part, (d, start, size) in enumerate(PARTS):

        @pl.when(c < CTX - d)
        def _():
            term_copy(part).wait_recv()

        @pl.when(c >= CTX - d)
        def _():
            rx[:, start : start + size] = jnp.zeros((2, size, HD), jnp.bfloat16)

    for w, ref in ((0, dk_ref), (1, dv_ref)):
        own_sum = acc[w, 2 * TOK : 3 * TOK, :]
        if w == 0:
            own_sum = own_sum * SCALING
        far = rx[w, 0:TOK].astype(jnp.float32)
        near = rx[w, TOK : 2 * TOK].astype(jnp.float32)
        ref[...] = (own_sum + near + far).astype(jnp.bfloat16)

    for dz, dc in partners:
        key_copy(partner(dz, dc)).wait_send()
        query_copy(partner(dz, dc)).wait_send()
    @pl.when((p >= 14) & crossing)
    def _():
        for r in range(TP):
            if r != 6:
                relay_copy(r).wait_send()

    @pl.when((p == 15) & crossing)
    def _():
        relay_copy(6).wait_send()

    @pl.when(crossing)
    def _():
        cross_copy(relay).wait_send()

    @pl.when((p == 0) & (plane >= 1))
    def _():
        onward_copy().wait_send()

    for d in (1, 2):

        @pl.when(p < PLANE - d)
        def _():
            wait_window(w_send.at[d - 1])

    for part, (d, start, size) in enumerate(PARTS):

        @pl.when(c >= d)
        def _():
            term_copy(part).wait_send()


def hand_over(*refs):
    sources, results, held, come, gone = refs[:4], refs[4:8], refs[8:12], refs[12], refs[13]
    ins = [pltpu.make_async_copy(sources[i], held[i], come.at[i]) for i in range(4)]
    outs = [pltpu.make_async_copy(held[i], results[i], gone.at[i]) for i in range(4)]
    for copy in ins:
        copy.start()
    for copy, onward in zip(ins, outs):
        copy.wait()
        onward.start()
    for onward in outs:
        onward.wait()


def on_device(query, key_states, value_states, grad_out, segment_ids):
    vmem = pl.BlockSpec(memory_space=pltpu.VMEM)
    hbm = pl.BlockSpec(memory_space=pltpu.HBM)
    bf16, f32 = jnp.bfloat16, jnp.float32
    dma = pltpu.SemaphoreType.DMA
    shapes = (
            jax.ShapeDtypeStruct((TOK, GROUP * HD), bf16),
            jax.ShapeDtypeStruct((TOK, GROUP * HD), bf16),
            jax.ShapeDtypeStruct((TOK, HD), bf16),
            jax.ShapeDtypeStruct((TOK, HD), bf16),
    )
    results = pl.pallas_call(
        kernel,
        out_shape=shapes,
        in_specs=[hbm, hbm, hbm, hbm, hbm],
        out_specs=(vmem, vmem, vmem, vmem),
        scratch_shapes=[
            pltpu.VMEM((SUB, QH * HD), bf16),
            pltpu.VMEM((SUB, QH * HD), bf16),
            pltpu.VMEM((SUB, KVH * HD), bf16),
            pltpu.VMEM((SUB, KVH * HD), bf16),
            pltpu.VMEM((TP, 2, SUB, HD), bf16),
            pltpu.VMEM((TP, 2 * GROUP, SUB, HD), bf16),
            pltpu.VMEM((TP, 2 * GROUP, SUB, HD), bf16),
            pltpu.VMEM((2, 3 * TOK, HD), bf16),
            pltpu.VMEM((2, HD, 3 * TOK), bf16),
            pltpu.VMEM((3 * TOK, TILE), f32),
            pltpu.VMEM((TP, 8, HALF), f32),
            pltpu.VMEM((WIN, LANES), f32),
            pltpu.VMEM((WIN, LANES), bf16),
            pltpu.VMEM((WIN, LANES), bf16),
            pltpu.VMEM((HD, LANES), bf16),
            pltpu.VMEM((2, 3 * TOK, HD), f32),
            pltpu.VMEM((2, 2 * TOK, HD), bf16),
            pltpu.VMEM((2, 2 * TOK, HD), bf16),
        ]
        + [dma((4,))]
        + [dma((TP,))] * 4
        + [dma((3,)), dma((2,)), dma((4,)), dma((4,))]
        + [
            pltpu.VMEM((CTX * TOK // TILE, TILE), jnp.int32),
            pltpu.VMEM((2, SUB, HD), bf16),
            dma,
            dma((TP,)),
            dma,
            dma,
            dma((PLANE,)),
        ],
        compiler_params=pltpu.CompilerParams(
            collective_id=0, has_side_effects=True, vmem_limit_bytes=56 * 2**20
        ),
        cost_estimate=pl.CostEstimate(
            flops=2 * 6 * UNITS * LANES * WIN * HD,
            bytes_accessed=4 * TOK * GROUP * HD * 2,
            transcendentals=UNITS * LANES * WIN,
        ),
        name="attention",
    )(query, key_states, value_states, grad_out, segment_ids.reshape(-1, TILE))
    whole = pl.BlockSpec(memory_space=pl.ANY)
    return pl.pallas_call(
        hand_over,
        out_shape=shapes,
        in_specs=[whole] * 4,
        out_specs=(whole,) * 4,
        scratch_shapes=[pltpu.VMEM(shape.shape, shape.dtype) for shape in shapes]
        + [dma((4,)), dma((4,))],
        compiler_params=pltpu.CompilerParams(vmem_limit_bytes=56 * 2**20),
        name="hand_over",
    )(*results)


def solution(mesh):
    in_specs = (
        P(("ctx", "tp"), None),
        P(("ctx", "tp"), None),
        P(("ctx", "tp"), None),
        P(("ctx", "tp"), None),
        P(),
    )
    out_specs = (P("ctx", "tp"), P("ctx", "tp"), P("ctx", "tp"), P("ctx", "tp"))
    return jax.shard_map(
        on_device, mesh=mesh, in_specs=in_specs, out_specs=out_specs, check_vma=False
    )
```

```python
import math

import jax
import jax.numpy as jnp
from jax import lax
from jax.experimental import pallas as pl
from jax.experimental.pallas import tpu as pltpu
from jax.sharding import PartitionSpec as P

QH = 32
KVH = 8
HD = 128
TOK = 512
SUB = 64
GROUP = QH // KVH
CTX = 64
PLANE = 16
PLANES = CTX // PLANE
EARLY = 5
TP = 8
HALF = SUB * GROUP
LANES = 2 * HALF
UNITS = TP // 2
WIN = 1152
TILE = 128
TILES = WIN // TILE
NEGATIVE = -1e30
MESH = pl.DeviceIdType.MESH
SCALING = HD**-0.5
EXP_SCALE = SCALING * math.log2(math.e)

PARTS = ((2, 0, 256), (2, 256, 256), (1, 512, 256), (1, 768, 256))

NT = (((1,), (1,)), ((), ()))


def dot(a, b):
    return jnp.dot(a, b, preferred_element_type=jnp.float32)


def dot_nt(a, b):
    return lax.dot_general(a, b, NT, preferred_element_type=jnp.float32)


def fold(x, op):
    parts = [x[i * 8 : (i + 1) * 8] for i in range(x.shape[0] // 8)]
    while len(parts) > 1:
        parts = [op(parts[i], parts[i + 1]) for i in range(0, len(parts), 2)]
    return parts[0]


def kernel(
    q_in,
    k_in,
    v_in,
    g_in,
    seg_in,
    out_ref,
    dq_ref,
    dk_ref,
    dv_ref,
    q_vm,
    g_vm,
    k_vm,
    v_vm,
    kv_out,
    qg_out,
    qg,
    kv,
    kvt,
    segcol,
    segrow,
    s_scr,
    p_scr,
    e_scr,
    gst_scr,
    acc,
    tx,
    rx,
    load_sem,
    q_send,
    q_recv,
    k_send,
    k_recv,
    w_send,
    w_recv,
    t_send,
    t_recv,
    seg,
    relay,
    seg_sem,
    r_send,
    r_recv,
    x_send,
    x_recv,
):
    c = lax.axis_index("ctx")
    t = lax.axis_index("tp")
    zh, co = t // 2, t % 2
    plane, p = c // PLANE, c % PLANE

    seg_copy = pltpu.make_async_copy(seg_in, seg, seg_sem)
    seg_copy.start()
    loads = [
        pltpu.make_async_copy(k_in, k_vm, load_sem.at[0]),
        pltpu.make_async_copy(v_in, v_vm, load_sem.at[1]),
        pltpu.make_async_copy(q_in, q_vm, load_sem.at[2]),
        pltpu.make_async_copy(g_in, g_vm, load_sem.at[3]),
    ]
    for load in loads:
        load.start()

    barrier = pltpu.get_barrier_semaphore()
    for d in range(1, TP):
        pl.semaphore_signal(barrier, inc=1, device_id={"tp": (t + d) % TP}, device_id_type=MESH)
    for d in (1, 2, CTX - 1, CTX - 2):
        pl.semaphore_signal(barrier, inc=1, device_id={"ctx": (c + d) % CTX}, device_id_type=MESH)

    crossing = plane < PLANES - 1

    def greet(block, to=t):
        pl.semaphore_signal(
            barrier, inc=1, device_id={"ctx": block, "tp": to}, device_id_type=MESH
        )

    first = plane * PLANE

    @pl.when(p < 8)
    def _():
        greet(first + 15)

    @pl.when((p >= 8) & (p != 14))
    def _():
        greet(first + 14)

    @pl.when(p == 15)
    def _():
        for r in range(TP):
            greet(first + r)

    @pl.when(p == 14)
    def _():
        for r in range(TP):
            if r != 6:
                greet(first + 8 + r)

    @pl.when((p == 0) & (plane >= 1))
    def _():
        for r in range(TP):
            greet(first - PLANE + t, r)
            greet(first - PLANE + 8 + t, r)

    arrivals = (
        TP - 1 + 4 + jnp.where(p < 14, 1, jnp.where(p == 14, 7, 9)) + jnp.where(crossing, 1, 0)
    )

    def own_rows(j):
        return pl.ds(pl.multiple_of(2 * TOK + j * SUB, SUB), SUB)

    for load in loads:
        load.wait()
    for j in range(TP):
        kv_out[j, 0] = k_vm[:, j * HD : (j + 1) * HD]
        kv_out[j, 1] = v_vm[:, j * HD : (j + 1) * HD]
    for j in range(TP):
        for h in range(GROUP):
            at = (j * GROUP + h) * HD
            qg_out[j, h] = q_vm[:, at : at + HD]
            qg_out[j, GROUP + h] = g_vm[:, at : at + HD]

    kv[:, own_rows(t), :] = kv_out[t]
    qg[t] = qg_out[t]

    pl.semaphore_wait(barrier, arrivals)

    def partner(dz, dc):
        return ((zh + dz) % 4) * 2 + (co + dc) % 2

    partners = [(1, 0), (3, 0), (1, 1), (3, 1), (2, 0), (2, 1), (0, 1)]
    across, below, above = (zh + 2) % 4, (zh + 3) % 4, (zh + 1) % 4
    targets = [zh * 2 + 1 - co, across * 2 + co, across * 2 + 1 - co]
    targets += [below * 2 + co, above * 2 + co, below * 2 + 1 - co, above * 2 + 1 - co]

    def exchange(src, dst, send, recv, to):
        return pltpu.make_async_remote_copy(
            src_ref=src,
            dst_ref=dst,
            send_sem=send.at[to],
            recv_sem=recv.at[t],
            device_id={"tp": to},
            device_id_type=MESH,
        )

    def key_copy(to):
        return exchange(kv_out.at[to], kv.at[:, own_rows(t)], k_send, k_recv, to)

    def query_copy(to):
        return exchange(qg_out.at[to], qg.at[t], q_send, q_recv, to)

    def relay_copy(r):
        return pltpu.make_async_remote_copy(
            src_ref=kv_out.at[r],
            dst_ref=relay,
            send_sem=r_send.at[r],
            recv_sem=r_recv,
            device_id={"ctx": first + r + 8 * (15 - p)},
            device_id_type=MESH,
        )

    def cross_copy(src):
        at = jnp.where(p < 8, TOK, 0) + t * SUB
        return pltpu.make_async_remote_copy(
            src_ref=src,
            dst_ref=kv.at[:, pl.ds(pl.multiple_of(at, SUB), SUB)],
            send_sem=x_send,
            recv_sem=x_recv.at[jnp.where(p < 8, 0, 8) + t],
            device_id={"ctx": (plane + 1) % PLANES * PLANE, "tp": p % 8},
            device_id_type=MESH,
        )

    @pl.when((p == 15) & crossing)
    def _():
        for r in range(TP):
            relay_copy(r).start()

    @pl.when((p == 14) & crossing)
    def _():
        for r in range(TP):
            if r != 6:
                relay_copy(r).start()
        cross_copy(kv_out.at[6]).start()

    for dz, dc in partners:
        key_copy(partner(dz, dc)).start()

    @pl.when((p != 14) & crossing)
    def _():
        pltpu.make_async_copy(relay, relay, r_recv).wait()
        cross_copy(relay).start()

    for to in targets[:EARLY]:
        query_copy(to).start()

    @pl.when(c < 1)
    def _():
        kv[:, TOK : 2 * TOK] = jnp.zeros((2, TOK, HD), jnp.bfloat16)

    @pl.when(c < 2)
    def _():
        kv[:, 0:TOK] = jnp.zeros((2, TOK, HD), jnp.bfloat16)

    acc[...] = jnp.zeros_like(acc)

    seg_copy.wait()
    for block in range(3):
        at = jnp.maximum(c - 2 + block, 0)
        rows = seg[pl.ds(pl.multiple_of(at * 4, 4), 4), :].astype(jnp.float32)
        rows = jnp.where(c - 2 + block >= 0, rows, -1.0)
        for i in range(4):
            wide_row = jnp.broadcast_to(rows[i : i + 1], (TILE, TILE))
            start = block * TOK + i * TILE
            segcol[start : start + TILE, :] = wide_row.T
    own = seg[pl.ds(pl.multiple_of(c * 4, 4), 4), :].astype(jnp.float32)
    low_lane = lax.broadcasted_iota(jnp.int32, (8, TILE), 1) < SUB
    for i in range(4):
        row = jnp.broadcast_to(own[i : i + 1], (8, TILE))
        turned = pltpu.roll(row, SUB, 1)
        low = jnp.where(low_lane, row, turned)
        high = jnp.where(low_lane, turned, row)
        segrow[2 * i] = jnp.concatenate([low, low], 1)
        segrow[2 * i + 1] = jnp.concatenate([high, high], 1)

    def window_copy(d, j):
        return pltpu.make_async_remote_copy(
            src_ref=kv.at[:, own_rows(j)],
            dst_ref=kv.at[:, pl.ds(pl.multiple_of((2 - d) * TOK + j * SUB, SUB), SUB)],
            send_sem=w_send.at[d - 1],
            recv_sem=w_recv.at[d - 1],
            device_id={"ctx": (c + d) % CTX},
            device_id_type=MESH,
        )

    def wait_window(sem):
        pltpu.make_async_copy(kv.at[:, pl.ds(0, TOK)], kv.at[:, pl.ds(0, TOK)], sem).wait()

    def send_window(j):
        for d in (1, 2):

            @pl.when(p < PLANE - d)
            def _():
                window_copy(d, j).start()

    send_window(t)
    for dz, dc in [(0, 1)] + partners[:-1]:
        j = partner(dz, dc)
        rows = kv.at[:, own_rows(j)]
        pltpu.make_async_copy(rows, rows, k_recv.at[j]).wait()
        send_window(j)

    def wait_cross(column):
        chunk = kv.at[:, pl.ds(0, SUB)]
        pltpu.make_async_copy(chunk, chunk, x_recv.at[column]).wait()

    def onward_copy():
        return pltpu.make_async_remote_copy(
            src_ref=kv.at[:, pl.ds(TOK, TOK)],
            dst_ref=kv.at[:, pl.ds(0, TOK)],
            send_sem=w_send.at[2],
            recv_sem=w_recv.at[1],
            device_id={"ctx": (c + 1) % CTX},
            device_id_type=MESH,
        )

    def turn(start):
        for i in range(TOK // TILE):
            at = start + i * TILE
            for w in range(2):
                block = kv[w, at : at + TILE, :].astype(jnp.float32)
                kvt[w, :, at : at + TILE] = block.T.astype(jnp.bfloat16)

    turn(2 * TOK)

    @pl.when((p == 0) & (plane >= 1))
    def _():
        for column in range(8):
            wait_cross(column)
        onward_copy().start()
        for column in range(8, 16):
            wait_cross(column)

    for d in (1, 2):

        @pl.when((p >= 1) & (c >= d))
        def _():
            wait_window(w_recv.at[d - 1])

        if d == 2:
            for to in targets[EARLY:]:
                query_copy(to).start()
        turn((2 - d) * TOK)

    lane = lax.broadcasted_iota(jnp.int32, (TILE, HALF), 1) % SUB
    place = lax.broadcasted_iota(jnp.int32, (TILE, HALF), 0)

    def term_copy(part):
        d, start, size = PARTS[part]
        return pltpu.make_async_remote_copy(
            src_ref=tx.at[:, pl.ds(start, size)],
            dst_ref=rx.at[:, pl.ds(start, size)],
            send_sem=t_send.at[part],
            recv_sem=t_recv.at[part],
            device_id={"ctx": (c + CTX - d) % CTX},
            device_id_type=MESH,
        )

    def send_terms(part):
        d, start, size = PARTS[part]
        tx[0, start : start + size] = (acc[0, start : start + size] * SCALING).astype(jnp.bfloat16)
        tx[1, start : start + size] = acc[1, start : start + size].astype(jnp.bfloat16)

        @pl.when(c >= d)
        def _():
            term_copy(part).start()

    outer = (zh == 0) | (zh == 3)

    def unit(i, final):
        dz = jnp.where(i < 2, i * 2, jnp.where((i == 2) == outer, 1, 3))
        sz = (zh + dz) % 4

        def arrived(j):
            pltpu.make_async_copy(qg.at[j], qg.at[j], q_recv.at[j]).wait()

        base = pl.multiple_of(sz * TILE, TILE)
        window = pl.ds(base, WIN)
        halves = [slice(0, HALF), slice(HALF, LANES)]

        def keys(n):
            return pl.ds(pl.multiple_of(base + n * TILE, TILE), TILE)

        def tile(n):
            return slice(n * TILE, (n + 1) * TILE)

        terms = []
        for half, at in enumerate(halves):
            j = sz * 2 + half
            if final:
                arrived(j)
            else:
                pl.when((i > 0) | (co != half))(lambda: arrived(j))
            qs = qg[j, :GROUP].reshape(HALF, HD)
            gs = qg[j, GROUP:].reshape(HALF, HD)
            seg_q = segrow[j][0:1]
            causal = place <= lane + half * SUB
            peak = None
            for n in range(TILES):
                s = dot_nt(kv[0, keys(n), :], qs)
                seg_k = segcol[keys(n), :]
                allowed = jnp.concatenate([seg_k, seg_k], 1) == seg_q
                if n == TILES - 1:
                    allowed = allowed & causal
                s = jnp.where(allowed, s, NEGATIVE)
                s_scr[tile(n), at] = s
                here = fold(s, jnp.maximum)
                peak = here if peak is None else jnp.maximum(peak, here)
            peak = jnp.max(peak, axis=0, keepdims=True) * EXP_SCALE

            total = None
            for n in range(TILES):
                p = jnp.exp2(s_scr[tile(n), at] * EXP_SCALE - peak)
                p_scr[tile(n), at] = p.astype(jnp.bfloat16)
                here = fold(p, jnp.add)
                total = here if total is None else total + here
            inverse = 1.0 / jnp.sum(total, axis=0, keepdims=True)

            attended = dot(kvt[1, :, window], p_scr[:, at]) * inverse
            gst = (gs.astype(jnp.float32).T * inverse).astype(jnp.bfloat16)
            delta = jnp.sum(gst.astype(jnp.float32) * attended, axis=0, keepdims=True)
            gst_scr[:, at] = gst
            terms.append((attended, gst, delta))

        qs = qg[pl.ds(sz * 2, 2), :GROUP].reshape(LANES, HD)

        def store(ref, half, value):
            value = value.T.astype(jnp.bfloat16)
            rows = pl.ds(pl.multiple_of(base + half * SUB, SUB), SUB)
            for h in range(GROUP):
                ref[rows, h * HD : (h + 1) * HD] = value[h * SUB : (h + 1) * SUB]

        for n in range(TILES):
            for half, at in enumerate(halves):
                attended, gst, delta = terms[half]
                slope = dot(kv[1, keys(n), :], gst)
                p = p_scr[tile(n), at].astype(jnp.float32)
                e_scr[tile(n), at] = (p * (slope - delta)).astype(jnp.bfloat16)
            acc[0, keys(n), :] += dot(e_scr[tile(n), :], qs)
            acc[1, keys(n), :] += dot_nt(p_scr[tile(n), :], gst_scr[...])
            if final and n in (3, 5, 7):
                send_terms(n // 2)
        for half, at in enumerate(halves):
            store(out_ref, half, terms[half][0])
            store(dq_ref, half, dot(kvt[0, :, window], e_scr[:, at]) * SCALING)

    def one_unit(i, carry):
        unit(i, False)
        return carry

    lax.fori_loop(0, UNITS - 1, one_unit, 0)

    send_terms(0)
    unit(UNITS - 1, True)

    for part, (d, start, size) in enumerate(PARTS):

        @pl.when(c < CTX - d)
        def _():
            term_copy(part).wait_recv()

        @pl.when(c >= CTX - d)
        def _():
            rx[:, start : start + size] = jnp.zeros((2, size, HD), jnp.bfloat16)

    for w, ref in ((0, dk_ref), (1, dv_ref)):
        own_sum = acc[w, 2 * TOK : 3 * TOK, :]
        if w == 0:
            own_sum = own_sum * SCALING
        far = rx[w, 0:TOK].astype(jnp.float32)
        near = rx[w, TOK : 2 * TOK].astype(jnp.float32)
        ref[...] = (own_sum + near + far).astype(jnp.bfloat16)

    for dz, dc in partners:
        key_copy(partner(dz, dc)).wait_send()
        query_copy(partner(dz, dc)).wait_send()
    @pl.when((p >= 14) & crossing)
    def _():
        for r in range(TP):
            if r != 6:
                relay_copy(r).wait_send()

    @pl.when((p == 15) & crossing)
    def _():
        relay_copy(6).wait_send()

    @pl.when(crossing)
    def _():
        cross_copy(relay).wait_send()

    @pl.when((p == 0) & (plane >= 1))
    def _():
        onward_copy().wait_send()

    for d in (1, 2):

        @pl.when(p < PLANE - d)
        def _():
            wait_window(w_send.at[d - 1])

    for part, (d, start, size) in enumerate(PARTS):

        @pl.when(c >= d)
        def _():
            term_copy(part).wait_send()


def hand_over(*refs):
    sources, results, held, come, gone = refs[:4], refs[4:8], refs[8:12], refs[12], refs[13]
    ins = [pltpu.make_async_copy(sources[i], held[i], come.at[i]) for i in range(4)]
    outs = [pltpu.make_async_copy(held[i], results[i], gone.at[i]) for i in range(4)]
    for copy in ins:
        copy.start()
    for copy, onward in zip(ins, outs):
        copy.wait()
        onward.start()
    for onward in outs:
        onward.wait()


def on_device(query, key_states, value_states, grad_out, segment_ids):
    vmem = pl.BlockSpec(memory_space=pltpu.VMEM)
    hbm = pl.BlockSpec(memory_space=pltpu.HBM)
    bf16, f32 = jnp.bfloat16, jnp.float32
    dma = pltpu.SemaphoreType.DMA
    shapes = (
            jax.ShapeDtypeStruct((TOK, GROUP * HD), bf16),
            jax.ShapeDtypeStruct((TOK, GROUP * HD), bf16),
            jax.ShapeDtypeStruct((TOK, HD), bf16),
            jax.ShapeDtypeStruct((TOK, HD), bf16),
    )
    results = pl.pallas_call(
        kernel,
        out_shape=shapes,
        in_specs=[hbm, hbm, hbm, hbm, hbm],
        out_specs=(vmem, vmem, vmem, vmem),
        scratch_shapes=[
            pltpu.VMEM((SUB, QH * HD), bf16),
            pltpu.VMEM((SUB, QH * HD), bf16),
            pltpu.VMEM((SUB, KVH * HD), bf16),
            pltpu.VMEM((SUB, KVH * HD), bf16),
            pltpu.VMEM((TP, 2, SUB, HD), bf16),
            pltpu.VMEM((TP, 2 * GROUP, SUB, HD), bf16),
            pltpu.VMEM((TP, 2 * GROUP, SUB, HD), bf16),
            pltpu.VMEM((2, 3 * TOK, HD), bf16),
            pltpu.VMEM((2, HD, 3 * TOK), bf16),
            pltpu.VMEM((3 * TOK, TILE), f32),
            pltpu.VMEM((TP, 8, HALF), f32),
            pltpu.VMEM((WIN, LANES), f32),
            pltpu.VMEM((WIN, LANES), bf16),
            pltpu.VMEM((WIN, LANES), bf16),
            pltpu.VMEM((HD, LANES), bf16),
            pltpu.VMEM((2, 3 * TOK, HD), f32),
            pltpu.VMEM((2, 2 * TOK, HD), bf16),
            pltpu.VMEM((2, 2 * TOK, HD), bf16),
        ]
        + [dma((4,))]
        + [dma((TP,))] * 4
        + [dma((3,)), dma((2,)), dma((4,)), dma((4,))]
        + [
            pltpu.VMEM((CTX * TOK // TILE, TILE), jnp.int32),
            pltpu.VMEM((2, SUB, HD), bf16),
            dma,
            dma((TP,)),
            dma,
            dma,
            dma((PLANE,)),
        ],
        compiler_params=pltpu.CompilerParams(
            collective_id=0, has_side_effects=True, vmem_limit_bytes=56 * 2**20
        ),
        cost_estimate=pl.CostEstimate(
            flops=2 * 6 * UNITS * LANES * WIN * HD,
            bytes_accessed=4 * TOK * GROUP * HD * 2,
            transcendentals=UNITS * LANES * WIN,
        ),
        name="attention",
    )(query, key_states, value_states, grad_out, segment_ids.reshape(-1, TILE))
    whole = pl.BlockSpec(memory_space=pl.ANY)
    return pl.pallas_call(
        hand_over,
        out_shape=shapes,
        in_specs=[whole] * 4,
        out_specs=(whole,) * 4,
        scratch_shapes=[pltpu.VMEM(shape.shape, shape.dtype) for shape in shapes]
        + [dma((4,)), dma((4,))],
        compiler_params=pltpu.CompilerParams(vmem_limit_bytes=56 * 2**20),
        name="hand_over",
    )(*results)


def solution(mesh):
    in_specs = (
        P(("ctx", "tp"), None),
        P(("ctx", "tp"), None),
        P(("ctx", "tp"), None),
        P(("ctx", "tp"), None),
        P(),
    )
    out_specs = (P("ctx", "tp"), P("ctx", "tp"), P("ctx", "tp"), P("ctx", "tp"))
    return jax.shard_map(
        on_device, mesh=mesh, in_specs=in_specs, out_specs=out_specs, check_vma=False
    )
```
